256 devices in a mesh: leaf: 16 (over z, core), grp: 16 (over y, x).
Axes of the slice: x: 4, y: 4, z: 8, core: 2. Of those that a mesh axis runs over, the one named last changes fastest.
Arguments:
- kept_inverse: bfloat16 [16384, 16384], P('leaf', 'grp'), may hold values from -6 to 6
- owner_map: int32 [64], replicated, may hold values from 0 to 63, as said below
- structure: int32 [2, 16, 16], replicated, may hold values from 0 to 63, as said below
- l_panel: bfloat16 [2, 65536, 256], P(None, ('leaf', 'grp')), may hold values from -0.09375 to 0.09375
- diag_inverse: float32 [2, 4096, 256], P(None, ('leaf', 'grp')), may hold values from -6 to 6
Outputs:
- offdiag: bfloat16 [2, 65536, 256], P(None, ('leaf', 'grp'))
- diag_block: float32 [2, 4096, 256], P(None, ('leaf', 'grp'))
The draws below stay inside these ranges and needn't reach their ends.
Inputs may be any that keep to these rules, and one draw needn't show every extreme that they name: `owner_map`: each ancestor has its own slot. `structure`: each supernode's 16 ancestors are distinct, in no particular order, and exactly one of them has owner_map // 4 equal to each index of leaf.
All inputs are finite; a program needn't handle non-finite values.
Results may differ from the reference program's by a relative error of at most 0.012.
Values may be sent and summed in bfloat16 or wider, within the bound.
A program may use at most 128 MiB of HBM per device.

```python
import jax
import jax.numpy as jnp
from jax import lax

NB = 256
SUPER = 2
ROWS_OWN = 4
NA = 64
ANC = 16
N_LEAF = 16


def slot_table(key):
    return jax.random.permutation(key, NA).astype(jnp.int32)


def draw_owner_map(key, part):
    positions = slot_table(key)
    return positions


def draw_structure(key, part):
    positions = slot_table(key)
    key = jax.random.fold_in(key, 7)
    inverse_slots = jnp.argsort(positions, stable=True).astype(jnp.int32)
    picks = jax.random.randint(jax.random.fold_in(key, 1), (SUPER, ANC, ANC), 0, ROWS_OWN)
    owners = jnp.arange(ANC, dtype=jnp.int32)
    slots = owners[None, None, :] * ROWS_OWN + picks
    members = jnp.take(inverse_slots, slots)
    row_keys = jax.random.split(jax.random.fold_in(key, 2), SUPER * ANC)
    orders = jax.vmap(lambda one_key: jax.random.permutation(one_key, ANC))(row_keys).reshape(SUPER, ANC, ANC)
    return jnp.take_along_axis(members, orders.astype(jnp.int32), axis=2).astype(jnp.int32)


def level_of(stream_key, dims, cuts, least, high):
    factor_of = 1.0
    for axis_at, shards_of in cuts:
        draws = jax.random.uniform(jax.random.fold_in(jax.random.fold_in(stream_key, 6), axis_at), (shards_of,), jnp.float32, least / len(cuts), high / len(cuts))
        factor_of = factor_of * jnp.repeat(jnp.exp(draws), dims[axis_at] // shards_of).reshape((-1,) + (1,) * (len(dims) - 1 - axis_at))
    return factor_of


def bell_draw(stream_key, extent, deviation, reach, cuts=(), kind=jnp.bfloat16):
    values = deviation * jax.random.normal(stream_key, extent, jnp.float32)
    if cuts:
        values = values * level_of(stream_key, extent, cuts, -0.22, 0.18)
    return jnp.clip(values, -reach, reach).astype(kind)


def setup_inputs(seed: int = 0) -> dict:
    key_of = jax.random.split(jax.random.key(seed), 6)
    kept_inverse = bell_draw(key_of[0], (NA * NB, NA * NB), 1.0, 6.0, ((0, 16), (1, 16)))
    owner_map = draw_owner_map(jax.random.fold_in(key_of[5], 71), 0)
    structure = draw_structure(jax.random.fold_in(key_of[5], 71), 0)
    l_panel = bell_draw(key_of[3], (SUPER, N_LEAF * ANC * NB, NB), (ANC * NB) ** -0.5, 0.09375, ((1, 256),))
    diag_inverse = bell_draw(key_of[4], (SUPER, N_LEAF * NB, NB), 1.0, 6.0, ((1, 256),), jnp.float32)
    return {"kept_inverse": kept_inverse, "owner_map": owner_map, "structure": structure, "l_panel": l_panel, "diag_inverse": diag_inverse}


def reference(kept_inverse, owner_map, structure, l_panel, diag_inverse):
    blocks = kept_inverse.reshape(NA, NB, NA, NB)

    def one_leaf(inputs):
        members, panel_rows, inverse = inputs
        slots = jnp.take(owner_map, members)
        chosen = jnp.take(jnp.take(blocks, slots, axis=0), slots, axis=2).reshape(ANC * NB, ANC * NB)
        block_rows = (-jnp.dot(chosen, panel_rows, preferred_element_type=jnp.float32)).astype(jnp.bfloat16)
        diag_out = inverse - jnp.dot(panel_rows.T, block_rows, preferred_element_type=jnp.float32)
        return block_rows, diag_out

    below = []
    diagonal = []
    for supernode in range(SUPER):
        block_rows, diag_out = lax.map(one_leaf, (structure[supernode], l_panel[supernode].reshape(N_LEAF, ANC * NB, NB), diag_inverse[supernode].reshape(N_LEAF, NB, NB)))
        below.append(block_rows.reshape(N_LEAF * ANC * NB, NB))
        diagonal.append(diag_out.reshape(N_LEAF * NB, NB))
    return jnp.stack(below, axis=0), jnp.stack(diagonal, axis=0)
```

```python
import jax
import jax.numpy as jnp
from jax import lax
from jax.experimental import pallas as pl
from jax.experimental.pallas import tpu as pltpu
from jax.sharding import PartitionSpec as P

MESH = pl.DeviceIdType.MESH
F32 = jnp.float32
BF16 = jnp.bfloat16


def kernel(
    owner, structure, stored, l_panel, diag_inverse,
    off_out, diag_out,
    blocks, slices, stage, panels, products, halves, sums, parts, parts_in, finals, rows, chosen, update, update_in,
    own_table, k_table, block_table,
    in_sem, p1_send, p1_recv, p2_send, p2_recv, ring_send, ring_recv, sib_send, sib_recv,
    half_send, half_recv, sum_send, sum_recv, part_send, part_recv, row_send, row_recv,
    off_send, off_recv, upd_send, upd_recv,
):
    leaf = lax.axis_index("leaf")
    grp = lax.axis_index("grp")
    z, core = leaf // 2, leaf % 2
    y, x = grp // 4, grp % 4

    def send(src, dst, send_sem, recv_sem, to_leaf, to_grp):
        pltpu.make_async_remote_copy(
            src_ref=src, dst_ref=dst, send_sem=send_sem, recv_sem=recv_sem,
            device_id=(to_leaf, to_grp), device_id_type=MESH,
        ).start()

    def wait(ref, sem):
        pltpu.make_async_copy(ref, ref, sem).wait()

    for a in range(4):
        for b in range(4):
            pltpu.make_async_copy(
                stored.at[pl.ds(a * 256, 256), pl.ds(b * 256, 256)], blocks.at[a * 4 + b], in_sem
            ).start()
    barrier = pltpu.get_barrier_semaphore()

    def greet(d, carry):
        pl.semaphore_signal(barrier, inc=1, device_id=(leaf, (grp + d) % 16), device_id_type=MESH)
        pl.semaphore_signal(barrier, inc=1, device_id=((leaf + d) % 16, grp), device_id_type=MESH)
        return carry

    lax.fori_loop(1, 16, greet, 0)
    pl.semaphore_wait(barrier, 30)

    def send_slices(d, carry):
        to = (grp + d) % 16
        send(l_panel.at[:, pl.ds(pl.multiple_of(to * 16, 16), 16), :], slices.at[:, grp], p1_send, p1_recv, leaf, to)
        return carry

    lax.fori_loop(1, 16, send_slices, 0)
    pltpu.make_async_copy(
        l_panel.at[:, pl.ds(pl.multiple_of(grp * 16, 16), 16), :], slices.at[:, grp], p1_recv
    ).start()

    for s in range(2):
        for j in range(16):
            own_table[s * 16 + j] = owner[structure[s, leaf, j]] // 4

    def find_k(q, carry):
        for s in range(2):
            k = jnp.int32(0)
            for j in range(16):
                k = jnp.where(own_table[s * 16 + j] == q, j, k)
            k_table[s * 16 + q] = k
        return carry

    lax.fori_loop(0, 16, find_k, 0)
    wait(slices, p1_recv)

    for q in range(16):
        for s in range(2):
            stage[q, s] = slices[s, k_table[s * 16 + q]]

    def send_panels(d, carry):
        to = (grp + d) % 16
        send(stage.at[to], panels.at[leaf, :, grp], p2_send, p2_recv, leaf, to)
        return carry

    lax.fori_loop(1, 16, send_panels, 0)
    pltpu.make_async_copy(stage.at[grp], panels.at[leaf, :, grp], p2_recv).start()

    def find_block(i, carry):
        for s in range(2):
            row, col = jnp.int32(0), jnp.int32(0)
            for j in range(16):
                slot = owner[structure[s, i, j]]
                row = jnp.where(slot // 4 == leaf, slot % 4, row)
                col = jnp.where(slot // 4 == grp, slot % 4, col)
            block_table[s * 16 + i] = row * 4 + col
        return carry

    lax.fori_loop(0, 16, find_block, 0)
    wait(blocks, in_sem)
    wait(panels.at[leaf], p2_recv)

    def source_z(m):
        return (z + 8 + jnp.where(m % 2 == 1, -((m + 1) // 2), m // 2)) % 8

    def axis_peer(s, d):
        if s == 0:
            return y * 4 + (x + d) % 4
        return ((y + d) % 4) * 4 + x

    def other_peer(s, d):
        return axis_peer(1 - s, d)

    place = (x, y)

    def gather_and_multiply(m):
        from_z = source_z(m)
        for s in range(2):
            held = panels.at[2 * from_z + core, s]

            @pl.when(m > 0)
            def _():
                wait(held, ring_recv.at[m * 2 + s])

            up = (m == 0) | ((m % 2 == 1) & (m <= (5 if s == 0 else 3)))
            down = (m == 0) | ((m % 2 == 0) & (m <= (4 if s == 0 else 6)))

            @pl.when(up)
            def _():
                slot = jnp.where(m == 0, 1, m + 2)
                send(held, held, ring_send, ring_recv.at[slot * 2 + s], ((z + 1) % 8) * 2 + core, grp)

            @pl.when(down)
            def _():
                slot = jnp.where(m == 0, 2, jnp.minimum(m + 2, 7))
                send(held, held, ring_send, ring_recv.at[slot * 2 + s], ((z + 7) % 8) * 2 + core, grp)

            send(held, held, sib_send, sib_recv.at[m * 2 + s], 2 * z + 1 - core, grp)
        for e in range(2):
            from_leaf = 2 * from_z + (core + e) % 2
            for s in range(2):
                if e == 1:
                    wait(panels.at[from_leaf, s], sib_recv.at[m * 2 + s])
                block = blocks[block_table[s * 16 + from_leaf]]
                panel = panels[from_leaf, s].reshape(256, 256)
                product = jnp.dot(block, panel, preferred_element_type=F32).astype(BF16)
                for to in range(4):
                    for sub in range(4):
                        q = 4 * sub + to if s == 0 else 4 * to + sub
                        products[m * 2 + s, to, sub // 2, e, sub % 2] = product[q * 16 : q * 16 + 16, :]
        for s in range(2):
            i = m * 2 + s
            opposite = (place[s] + 2) % 4
            send(products.at[i, opposite, 0], halves.at[i, 0], half_send, half_recv.at[i], leaf, axis_peer(s, 1))
            send(products.at[i, opposite, 1], halves.at[i, 1], half_send, half_recv.at[i], leaf, axis_peer(s, 3))

    def add_halves(m):
        for s in range(2):
            i = m * 2 + s
            after, before = (place[s] + 1) % 4, (place[s] + 3) % 4
            wait(halves.at[i], half_recv.at[i])
            products[i, after, 0] = (products[i, after, 0].astype(F32) + halves[i, 0].astype(F32)).astype(BF16)
            send(products.at[i, after], sums.at[i, 0], sum_send, sum_recv.at[i], leaf, axis_peer(s, 1))
            products[i, before, 1] = (products[i, before, 1].astype(F32) + halves[i, 1].astype(F32)).astype(BF16)
            send(products.at[i, before], sums.at[i, 1], sum_send, sum_recv.at[i], leaf, axis_peer(s, 3))

    def add_sums(m):
        for s in range(2):
            i = m * 2 + s
            wait(sums.at[i], sum_recv.at[i])
            total = products[i, place[s]].astype(F32) + sums[i, 0].astype(F32) + sums[i, 1].astype(F32)
            total = total.astype(BF16)
            for to in range(4):
                for e in range(2):
                    parts[i, to, e] = total[to // 2, e, to % 2]
            for d in range(1, 4):
                to = (place[1 - s] + d) % 4
                send(parts.at[i, to], parts_in.at[i, d - 1], part_send, part_recv.at[i], leaf, other_peer(s, d))

    def add_parts(m):
        from_z = source_z(m)
        for s in range(2):
            i = m * 2 + s
            wait(parts_in.at[i, pl.ds(0, 3)], part_recv.at[i])
            total = parts[i, place[1 - s]].astype(F32)
            for d in range(3):
                total = total + parts_in[i, d].astype(F32)
            total = (-total).astype(BF16)
            for e in range(2):
                f = m * 4 + s * 2 + e
                finals[f] = total[e]
                to_leaf = 2 * from_z + (core + e) % 2
                if e == 0:

                    @pl.when(m == 0)
                    def _():
                        pltpu.make_async_copy(finals.at[f], rows.at[s, leaf], row_recv).start()

                    @pl.when(m > 0)
                    def _():
                        send(finals.at[f], rows.at[s, leaf], row_send, row_recv, to_leaf, grp)

                else:
                    send(finals.at[f], rows.at[s, leaf], row_send, row_recv, to_leaf, grp)

    def step(t, carry):
        pl.when(t < 8)(lambda: gather_and_multiply(t))
        pl.when((t >= 1) & (t < 9))(lambda: add_halves(t - 1))
        pl.when((t >= 2) & (t < 10))(lambda: add_sums(t - 2))
        pl.when(t >= 3)(lambda: add_parts(t - 3))
        return carry

    lax.fori_loop(0, 11, step, 0)

    wait(rows, row_recv)
    for j in range(16):
        for s in range(2):
            chosen[s, j] = rows[s, own_table[s * 16 + j]]

    def send_off(d, carry):
        to = (grp + d) % 16
        send(chosen.at[:, to], off_out.at[:, grp], off_send, off_recv, leaf, to)
        return carry

    lax.fori_loop(1, 16, send_off, 0)
    pltpu.make_async_copy(chosen.at[:, grp], off_out.at[:, grp], off_recv).start()

    for s in range(2):
        value = lax.dot_general(
            slices[s].reshape(256, 256), chosen[s].reshape(256, 256), (((0,), (0,)), ((), ())),
            preferred_element_type=F32,
        )
        update[s] = value.astype(BF16).reshape(16, 16, 256)

    def send_update(d, carry):
        to = (grp + d) % 16
        send(update.at[:, to], update_in.at[grp], upd_send, upd_recv, leaf, to)
        return carry

    lax.fori_loop(1, 16, send_update, 0)
    pltpu.make_async_copy(update.at[:, grp], update_in.at[grp], upd_recv).start()
    wait(update_in, upd_recv)
    total = update_in[0].astype(F32)
    for g in range(1, 16):
        total = total + update_in[g].astype(F32)
    diag_out[...] = diag_inverse[...] - total
    wait(off_out, off_recv)

    wait(slices.at[:, pl.ds(0, 15)], p1_send)
    wait(stage.at[pl.ds(0, 15)], p2_send)
    wait(panels.at[pl.ds(0, 7)], ring_send)
    wait(panels.at[pl.ds(0, 8)], sib_send)
    wait(halves, half_send)
    wait(sums, sum_send)
    wait(parts.at[pl.ds(0, 12)], part_send)
    wait(finals.at[pl.ds(0, 30)], row_send)
    wait(chosen.at[:, pl.ds(0, 15)], off_send)
    wait(update.at[:, pl.ds(0, 15)], upd_send)


def per_device(kept_inverse, owner_map, structure, l_panel, diag_inverse):
    any_space = pl.BlockSpec(memory_space=pl.ANY)
    vmem = pl.BlockSpec(memory_space=pltpu.VMEM)
    smem = pl.BlockSpec(memory_space=pltpu.SMEM)
    dma = pltpu.SemaphoreType.DMA
    off, diag = pl.pallas_call(
        kernel,
        out_shape=(
            jax.ShapeDtypeStruct((2, 16, 16, 256), BF16),
            jax.ShapeDtypeStruct((2, 16, 256), F32),
        ),
        in_specs=[smem, smem, any_space, any_space, vmem],
        out_specs=(any_space, vmem),
        scratch_shapes=[
            pltpu.VMEM((16, 256, 256), BF16),
            pltpu.VMEM((2, 16, 16, 256), BF16),
            pltpu.VMEM((16, 2, 16, 256), BF16),
            pltpu.VMEM((16, 2, 16, 16, 256), BF16),
            pltpu.VMEM((16, 4, 2, 2, 2, 16, 256), BF16),
            pltpu.VMEM((16, 2, 2, 2, 16, 256), BF16),
            pltpu.VMEM((16, 2, 2, 2, 2, 16, 256), BF16),
            pltpu.VMEM((16, 4, 2, 16, 256), BF16),
            pltpu.VMEM((16, 3, 2, 16, 256), BF16),
            pltpu.VMEM((32, 16, 256), BF16),
            pltpu.VMEM((2, 16, 16, 256), BF16),
            pltpu.VMEM((2, 16, 16, 256), BF16),
            pltpu.VMEM((2, 16, 16, 256), BF16),
            pltpu.VMEM((16, 2, 16, 256), BF16),
            pltpu.SMEM((32,), jnp.int32),
            pltpu.SMEM((32,), jnp.int32),
            pltpu.SMEM((32,), jnp.int32),
            dma, dma, dma, dma, dma,
            dma, dma((16,)), dma, dma((16,)),
            dma, dma((16,)), dma, dma((16,)), dma, dma((16,)),
            dma, dma, dma, dma, dma, dma,
        ],
        compiler_params=pltpu.CompilerParams(
            collective_id=0, has_side_effects=True, vmem_limit_bytes=48 * 1024 * 1024
        ),
    )(owner_map, structure, kept_inverse, l_panel, diag_inverse)
    return off.reshape(2, 256, 256), diag


def solution(mesh):
    in_specs = (
        P("leaf", "grp"),
        P(),
        P(),
        P(None, ("leaf", "grp"), None),
        P(None, ("leaf", "grp"), None),
    )
    out_specs = (P(None, ("leaf", "grp"), None), P(None, ("leaf", "grp"), None))
    return jax.shard_map(
        per_device, mesh=mesh, in_specs=in_specs, out_specs=out_specs, check_vma=False
    )
```

```python
import jax
import jax.numpy as jnp
from jax import lax
from jax.experimental import pallas as pl
from jax.experimental.pallas import tpu as pltpu
from jax.sharding import PartitionSpec as P

MESH = pl.DeviceIdType.MESH
F32 = jnp.float32
BF16 = jnp.bfloat16
VMEM_LIMIT = 60 * 1024 * 1024
LAG_HALVES, LAG_SUMS, LAG_PARTS = 3, 6, 9
DIRECT = 14
FARTHEST_FIRST = sorted(
    ((dy, dx) for dy in range(4) for dx in range(4) if dy or dx), key=lambda d: -(min(d[0], 4 - d[0]) + min(d[1], 4 - d[1]))
)


def rem(a, n):
    return lax.rem(a, jnp.int32(n))


def div(a, n):
    return lax.div(a, jnp.int32(n))


def kernel(
    owner_hbm, structure_hbm, stored, l_panel_hbm, diag_hbm,
    off_out, diag_out,
    blocks, slices_0, slices_1, stage, panels, products, halves, sums, parts, parts_in, finals, rows_0, rows_1, leaving, arriving,
    l_panel, diag_inverse, owner, structure, own_table, k_table, block_table,
    in_sem, table_sem, p1_send, p1_recv, p2_send, p2_recv, ring_send, ring_recv, sib_send, sib_recv,
    half_send, half_recv, sum_send_two, sum_send, sum_recv, part_send, part_recv, row_send, row_recv,
    end_send, end_recv,
):
    slices, rows = (slices_0, slices_1), (rows_0, rows_1)
    leaf = lax.axis_index("leaf")
    grp = lax.axis_index("grp")
    z, core = div(leaf, 2), rem(leaf, 2)
    y, x = div(grp, 4), rem(grp, 4)

    def send(src, dst, send_sem, recv_sem, to_leaf, to_grp):
        pltpu.make_async_remote_copy(
            src_ref=src, dst_ref=dst, send_sem=send_sem, recv_sem=recv_sem,
            device_id=(to_leaf, to_grp), device_id_type=MESH,
        ).start()

    def wait(ref, sem):
        pltpu.make_async_copy(ref, ref, sem).wait()

    barrier = pltpu.get_barrier_semaphore()
    pltpu.make_async_copy(l_panel_hbm, l_panel, table_sem.at[3]).start()
    peers = [rem(y + dy, 4) * 4 + rem(x + dx, 4) for dy, dx in FARTHEST_FIRST]
    for to in peers:
        pl.semaphore_signal(barrier, inc=1, device_id=(leaf, to), device_id_type=MESH)

    def greet(d, carry):
        pl.semaphore_signal(barrier, inc=1, device_id=(rem(leaf + d, 16), grp), device_id_type=MESH)
        return carry

    lax.fori_loop(1, 16, greet, 0)
    pltpu.make_async_copy(owner_hbm, owner, table_sem.at[0]).start()
    pltpu.make_async_copy(structure_hbm, structure, table_sem.at[1]).start()
    pltpu.make_async_copy(diag_hbm, diag_inverse, table_sem.at[2]).start()
    for a in range(4):
        for b in range(4):
            pltpu.make_async_copy(
                stored.at[pl.ds(a * 256, 256), pl.ds(b * 256, 256)], blocks.at[a * 4 + b], in_sem
            ).start()
    wait(l_panel, table_sem.at[3])
    pl.semaphore_wait(barrier, 30)

    def rows_of(r):
        return pl.ds(pl.multiple_of(r * 16, 16), 16)

    for s in range(2):
        for to in peers:
            send(l_panel.at[s, rows_of(to), :], slices[s].at[grp], p1_send.at[s], p1_recv.at[s], leaf, to)
        pltpu.make_async_copy(l_panel.at[s, rows_of(grp), :], slices[s].at[grp], p1_recv.at[s]).start()

    wait(owner, table_sem.at[0])
    wait(structure, table_sem.at[1])
    for s in range(2):
        for j in range(16):
            own_table[s * 16 + j] = owner[structure[s, leaf, j]] >> 2

    def find_k(q, carry):
        for s in range(2):
            k = jnp.int32(0)
            for j in range(16):
                k = jnp.where(own_table[s * 16 + j] == q, j, k)
            k_table[s * 16 + q] = k
        return carry

    lax.fori_loop(0, 16, find_k, 0)

    for s in range(2):
        wait(slices[s], p1_recv.at[s])
        for q in range(16):
            stage[s, q] = slices[s][k_table[s * 16 + q]]
        for to in peers:
            send(stage.at[s, to], panels.at[leaf, s, grp], p2_send.at[s], p2_recv.at[s], leaf, to)
        pltpu.make_async_copy(stage.at[s, grp], panels.at[leaf, s, grp], p2_recv.at[s]).start()

    def find_block(i, carry):
        for s in range(2):
            row, col = jnp.int32(0), jnp.int32(0)
            for j in range(16):
                slot = owner[structure[s, i, j]]
                held_by, pick = slot >> 2, slot & 3
                row = jnp.where(held_by == leaf, pick, row)
                col = jnp.where(held_by == grp, pick, col)
            block_table[s * 16 + i] = row * 4 + col
        return carry

    lax.fori_loop(0, 16, find_block, 0)
    wait(blocks, in_sem)

    def place_of(u):
        pair, turn = div(u + 2, 4), rem(u + 2, 4)
        m = jnp.where(u < 2, 0, jnp.where(u < 14, 2 * pair - 1 + rem(turn, 2), 7))
        s = jnp.where(u < 2, u, jnp.where(u < 14, div(turn, 2), u - 14))
        from_z = rem(z + 8 + jnp.where(rem(m, 2) == 1, -div(m + 1, 2), div(m, 2)), 8)
        return m, s, from_z

    def first_peer(s, d):
        return rem(y + s * d, 4) * 4 + rem(x + (1 - s) * d, 4)

    def second_peer(s, d):
        return first_peer(1 - s, d)

    def first_place(s):
        return x * (1 - s) + y * s

    def multiply(u, s, from_leaf, e):
        block = blocks[block_table[s * 16 + from_leaf]]
        panel = panels[from_leaf, s].reshape(256, 256)
        product = jnp.dot(block, panel, preferred_element_type=F32).astype(BF16)
        for q in range(16):
            to = (q % 4) * (1 - s) + (q // 4) * s
            sub = (q // 4) * (1 - s) + (q % 4) * s
            products[u, to, div(sub, 2), e, rem(sub, 2)] = product[q * 16 : q * 16 + 16, :]

    def gather(u):
        m, s, from_z = place_of(u)
        held = panels.at[2 * from_z + core, s]
        pl.when(m == 0)(lambda: wait(held, p2_recv.at[s]))
        for h in range(2):
            half = held.at[pl.ds(h * 8, 8)]
            pl.when(m > 0)(lambda: wait(half, ring_recv.at[m * 4 + s * 2 + h]))
            up = (m == 0) | ((rem(m, 2) == 1) & (m <= (5 if h == 0 else 3)))
            down = (m == 0) | ((rem(m, 2) == 0) & (m <= (4 if h == 0 else 6)))

            @pl.when(up)
            def _():
                slot = jnp.where(m == 0, 1, m + 2)
                send(half, half, ring_send, ring_recv.at[slot * 4 + s * 2 + h], rem(z + 1, 8) * 2 + core, grp)

            @pl.when(down)
            def _():
                slot = jnp.where(m == 0, 2, jnp.minimum(m + 2, 7))
                send(half, half, ring_send, ring_recv.at[slot * 4 + s * 2 + h], rem(z + 7, 8) * 2 + core, grp)

        send(held, held, sib_send, sib_recv.at[u], 2 * z + 1 - core, grp)
        multiply(u, s, 2 * from_z + core, 0)

    def multiply_other(u):
        m, s, from_z = place_of(u)
        from_leaf = 2 * from_z + 1 - core
        wait(panels.at[from_leaf, s], sib_recv.at[u])
        multiply(u, s, from_leaf, 1)
        opposite = rem(first_place(s) + 2, 4)

        @pl.when(u < DIRECT)
        def _():
            send(products.at[u, opposite, 0], halves.at[u, 0], half_send, half_recv.at[u], leaf, first_peer(s, 1))
            send(products.at[u, opposite, 1], halves.at[u, 1], half_send, half_recv.at[u], leaf, first_peer(s, 3))

        @pl.when(u >= DIRECT)
        def _():
            for d, slot in ((2, 2), (1, 0), (3, 1)):
                to = rem(first_place(s) + d, 4)
                send(products.at[u, to], sums.at[u, slot], sum_send, sum_recv.at[u], leaf, first_peer(s, d))

    def add_halves(u):
        m, s, from_z = place_of(u)
        after, before = rem(first_place(s) + 1, 4), rem(first_place(s) + 3, 4)
        wait(halves.at[u], half_recv.at[u])
        products[u, after, 0] = (products[u, after, 0].astype(F32) + halves[u, 0].astype(F32)).astype(BF16)
        send(products.at[u, after], sums.at[u, 0], sum_send_two, sum_recv.at[u], leaf, first_peer(s, 1))
        products[u, before, 1] = (products[u, before, 1].astype(F32) + halves[u, 1].astype(F32)).astype(BF16)
        send(products.at[u, before], sums.at[u, 1], sum_send_two, sum_recv.at[u], leaf, first_peer(s, 3))

    def add_sums(u, received):
        m, s, from_z = place_of(u)
        wait(sums.at[u, pl.ds(0, received)], sum_recv.at[u])
        total = products[u, first_place(s)].astype(F32)
        for slot in range(received):
            total = total + sums[u, slot].astype(F32)
        total = total.astype(BF16)
        for to in range(4):
            for e in range(2):
                parts[u, to, e] = total[to // 2, e, to % 2]
        for d in (2, 1, 3):
            to = rem(first_place(1 - s) + d, 4)
            send(parts.at[u, to], parts_in.at[u, d - 1], part_send, part_recv.at[u], leaf, second_peer(s, d))

    def add_parts(u):
        m, s, from_z = place_of(u)
        wait(parts_in.at[u], part_recv.at[u])
        total = parts[u, first_place(1 - s)].astype(F32)
        for d in range(3):
            total = total + parts_in[u, d].astype(F32)
        finals[u] = (-total).astype(BF16)

        def send_rows(s):
            @pl.when(m == 0)
            def _():
                pltpu.make_async_copy(finals.at[u, 0], rows[s].at[leaf], row_recv.at[s]).start()

            @pl.when(m > 0)
            def _():
                send(finals.at[u, 0], rows[s].at[leaf], row_send, row_recv.at[s], 2 * from_z + core, grp)

            send(finals.at[u, 1], rows[s].at[leaf], row_send, row_recv.at[s], 2 * from_z + 1 - core, grp)

        pl.when(s == 0)(lambda: send_rows(0))
        pl.when(s == 1)(lambda: send_rows(1))

    def step(t, carry):
        halved, summed, done = t - LAG_HALVES, t - LAG_SUMS, t - LAG_PARTS
        pl.when(t < 16)(lambda: gather(t))
        pl.when((halved >= 0) & (halved < DIRECT))(lambda: add_halves(halved))
        pl.when((summed >= 0) & (summed < DIRECT))(lambda: add_sums(summed, 2))
        pl.when((summed >= DIRECT) & (summed < 16))(lambda: add_sums(summed, 3))
        pl.when(done >= 0)(lambda: add_parts(done))
        pl.when(t < 16)(lambda: multiply_other(t))
        return carry

    lax.fori_loop(0, 16 + LAG_PARTS, step, 0)

    def send_end(kind, s):
        sem = end_recv.at[kind * (1 + s)]
        for to in peers:
            send(leaving.at[kind, s, to], arriving.at[kind, s, grp], end_send, sem, leaf, to)
        pltpu.make_async_copy(leaving.at[kind, s, grp], arriving.at[kind, s, grp], sem).start()

    def diag_part(s):
        value = lax.dot_general(
            slices[s][...].reshape(256, 256), leaving[0, s].reshape(256, 256), (((0,), (0,)), ((), ())),
            preferred_element_type=F32,
        )
        leaving[1, s] = value.astype(BF16).reshape(16, 16, 256)
        send_end(1, s)

    for s in range(2):
        wait(rows[s], row_recv.at[s])
        for j in range(16):
            leaving[0, s, j] = rows[s][own_table[s * 16 + j]]
        send_end(0, s)
    for s in range(2):
        diag_part(s)

    wait(diag_inverse, table_sem.at[2])
    wait(arriving.at[0], end_recv.at[0])
    off_out[...] = arriving[0]
    for s in range(2):
        wait(arriving.at[1, s], end_recv.at[1 + s])
        total = arriving[1, s, 0].astype(F32)
        for g in range(1, 16):
            total = total + arriving[1, s, g].astype(F32)
        diag_out[s] = diag_inverse[s] - total

    for s in range(2):
        wait(slices[s].at[pl.ds(0, 15)], p1_send.at[s])
        wait(stage.at[s, pl.ds(0, 15)], p2_send.at[s])
    wait(leaving.at[:, :, pl.ds(0, 15)], end_send)
    wait(panels.at[pl.ds(0, 7)], ring_send)
    wait(panels.at[pl.ds(0, 8)], sib_send)
    wait(halves.at[pl.ds(0, DIRECT)], half_send)
    wait(sums.at[pl.ds(0, DIRECT), pl.ds(0, 2)], sum_send_two)
    wait(sums.at[pl.ds(DIRECT, 16 - DIRECT)], sum_send)
    wait(parts_in, part_send)
    wait(finals.at[pl.ds(0, 15)], row_send)


def finish(off, diag, off_out, diag_out):
    off_out[...] = off[...]
    diag_out[...] = diag[...]


def per_device(kept_inverse, owner_map, structure, l_panel, diag_inverse):
    hbm = pl.BlockSpec(memory_space=pl.ANY)
    vmem = pl.BlockSpec(memory_space=pltpu.VMEM)
    dma = pltpu.SemaphoreType.DMA
    off, diag = pl.pallas_call(
        kernel,
        out_shape=(
            jax.ShapeDtypeStruct((2, 16, 16, 256), BF16),
            jax.ShapeDtypeStruct((2, 16, 256), F32),
        ),
        in_specs=[hbm] * 5,
        out_specs=(vmem, vmem),
        scratch_shapes=[
            pltpu.VMEM((16, 256, 256), BF16),
            pltpu.VMEM((16, 16, 256), BF16),
            pltpu.VMEM((16, 16, 256), BF16),
            pltpu.VMEM((2, 16, 16, 256), BF16),
            pltpu.VMEM((16, 2, 16, 16, 256), BF16),
            pltpu.VMEM((16, 4, 2, 2, 2, 16, 256), BF16),
            pltpu.VMEM((16, 2, 2, 2, 16, 256), BF16),
            pltpu.VMEM((16, 3, 2, 2, 2, 16, 256), BF16),
            pltpu.VMEM((16, 4, 2, 16, 256), BF16),
            pltpu.VMEM((16, 3, 2, 16, 256), BF16),
            pltpu.VMEM((16, 2, 16, 256), BF16),
            pltpu.VMEM((16, 16, 256), BF16),
            pltpu.VMEM((16, 16, 256), BF16),
            pltpu.VMEM((2, 2, 16, 16, 256), BF16),
            pltpu.VMEM((2, 2, 16, 16, 256), BF16),
            pltpu.VMEM((2, 256, 256), BF16),
            pltpu.VMEM((2, 16, 256), F32),
            pltpu.SMEM((64,), jnp.int32),
            pltpu.SMEM((2, 16, 16), jnp.int32),
            pltpu.SMEM((32,), jnp.int32),
            pltpu.SMEM((32,), jnp.int32),
            pltpu.SMEM((32,), jnp.int32),
            dma, dma((4,)), dma((2,)), dma((2,)), dma((2,)), dma((2,)),
            dma, dma((32,)), dma, dma((16,)),
            dma, dma((16,)), dma, dma, dma((16,)), dma, dma((16,)),
            dma, dma((2,)), dma, dma((3,)),
        ],
        compiler_params=pltpu.CompilerParams(
            collective_id=0, has_side_effects=True, vmem_limit_bytes=VMEM_LIMIT
        ),
    )(owner_map, structure, kept_inverse, l_panel, diag_inverse)
    off, diag = pl.pallas_call(
        finish,
        out_shape=(jax.ShapeDtypeStruct(off.shape, off.dtype), jax.ShapeDtypeStruct(diag.shape, diag.dtype)),
        in_specs=[vmem, vmem],
        out_specs=(vmem, vmem),
    )(off, diag)
    return off.reshape(2, 256, 256), diag


def solution(mesh):
    in_specs = (
        P("leaf", "grp"),
        P(),
        P(),
        P(None, ("leaf", "grp"), None),
        P(None, ("leaf", "grp"), None),
    )
    out_specs = (P(None, ("leaf", "grp"), None), P(None, ("leaf", "grp"), None))
    return jax.shard_map(
        per_device, mesh=mesh, in_specs=in_specs, out_specs=out_specs, check_vma=False
    )
```

```python
import jax
import jax.numpy as jnp
from jax import lax
from jax.experimental import pallas as pl
from jax.experimental.pallas import tpu as pltpu
from jax.sharding import PartitionSpec as P

MESH = pl.DeviceIdType.MESH
F32 = jnp.float32
BF16 = jnp.bfloat16
VMEM_LIMIT = 60 * 1024 * 1024
LAG_HALVES, LAG_SUMS, LAG_PARTS = 1, 3, 5
DIRECT = 14
FARTHEST_FIRST = sorted(
    ((dy, dx) for dy in range(4) for dx in range(4) if dy or dx), key=lambda d: -(min(d[0], 4 - d[0]) + min(d[1], 4 - d[1]))
)


def rem(a, n):
    return lax.rem(a, jnp.int32(n))


def div(a, n):
    return lax.div(a, jnp.int32(n))


def kernel(
    owner_hbm, structure_hbm, stored, l_panel_hbm, diag_hbm,
    off_out, diag_out,
    blocks, slices_0, slices_1, stage, panels, products, halves, sums, parts, parts_in, finals, rows_0, rows_1, leaving, arriving,
    l_panel, diag_inverse, owner, structure, own_table, k_table, block_table,
    in_sem, table_sem, p1_send, p1_recv, p2_send, p2_recv, ring_send, ring_recv, sib_send, sib_recv,
    half_send, half_recv, sum_send_two, sum_send, sum_recv, part_send, part_recv, row_send, row_recv,
    end_send, end_recv,
):
    slices, rows = (slices_0, slices_1), (rows_0, rows_1)
    leaf = lax.axis_index("leaf")
    grp = lax.axis_index("grp")
    z, core = div(leaf, 2), rem(leaf, 2)
    y, x = div(grp, 4), rem(grp, 4)

    def send(src, dst, send_sem, recv_sem, to_leaf, to_grp):
        pltpu.make_async_remote_copy(
            src_ref=src, dst_ref=dst, send_sem=send_sem, recv_sem=recv_sem,
            device_id=(to_leaf, to_grp), device_id_type=MESH,
        ).start()

    def wait(ref, sem):
        pltpu.make_async_copy(ref, ref, sem).wait()

    barrier = pltpu.get_barrier_semaphore()
    pltpu.make_async_copy(l_panel_hbm, l_panel, table_sem.at[3]).start()
    peers = [rem(y + dy, 4) * 4 + rem(x + dx, 4) for dy, dx in FARTHEST_FIRST]
    for to in peers:
        pl.semaphore_signal(barrier, inc=1, device_id=(leaf, to), device_id_type=MESH)

    def greet(d, carry):
        pl.semaphore_signal(barrier, inc=1, device_id=(rem(leaf + d, 16), grp), device_id_type=MESH)
        return carry

    lax.fori_loop(1, 16, greet, 0)
    pltpu.make_async_copy(owner_hbm, owner, table_sem.at[0]).start()
    pltpu.make_async_copy(structure_hbm, structure, table_sem.at[1]).start()
    pltpu.make_async_copy(diag_hbm, diag_inverse, table_sem.at[2]).start()
    for a in range(4):
        for b in range(4):
            pltpu.make_async_copy(
                stored.at[pl.ds(a * 256, 256), pl.ds(b * 256, 256)], blocks.at[a * 4 + b], in_sem
            ).start()
    wait(l_panel, table_sem.at[3])
    pl.semaphore_wait(barrier, 30)

    def rows_of(r):
        return pl.ds(pl.multiple_of(r * 16, 16), 16)

    def send_slices(s):
        for to in peers:
            send(l_panel.at[s, rows_of(to), :], slices[s].at[grp], p1_send.at[s], p1_recv.at[s], leaf, to)
        pltpu.make_async_copy(l_panel.at[s, rows_of(grp), :], slices[s].at[grp], p1_recv.at[s]).start()

    send_slices(0)

    wait(owner, table_sem.at[0])
    wait(structure, table_sem.at[1])
    for s in range(2):
        for j in range(16):
            own_table[s * 16 + j] = owner[structure[s, leaf, j]] >> 2

    def find_k(q, carry):
        for s in range(2):
            k = jnp.int32(0)
            for j in range(16):
                k = jnp.where(own_table[s * 16 + j] == q, j, k)
            k_table[s * 16 + q] = k
        return carry

    lax.fori_loop(0, 16, find_k, 0)
    send_slices(1)

    for s in range(2):
        wait(slices[s], p1_recv.at[s])
        for q in range(16):
            stage[s, q] = slices[s][k_table[s * 16 + q]]
        for to in peers:
            send(stage.at[s, to], panels.at[leaf, s, grp], p2_send.at[s], p2_recv.at[s], leaf, to)
        pltpu.make_async_copy(stage.at[s, grp], panels.at[leaf, s, grp], p2_recv.at[s]).start()

    def find_block(i, carry):
        for s in range(2):
            row, col = jnp.int32(0), jnp.int32(0)
            for j in range(16):
                slot = owner[structure[s, i, j]]
                held_by, pick = slot >> 2, slot & 3
                row = jnp.where(held_by == leaf, pick, row)
                col = jnp.where(held_by == grp, pick, col)
            block_table[s * 16 + i] = row * 4 + col
        return carry

    lax.fori_loop(0, 16, find_block, 0)
    wait(blocks, in_sem)

    def place_of(u):
        pair, turn = div(u + 2, 4), rem(u + 2, 4)
        m = jnp.where(u < 2, 0, jnp.where(u < 14, 2 * pair - 1 + rem(turn, 2), 7))
        s = jnp.where(u < 2, u, jnp.where(u < 14, div(turn, 2), u - 14))
        from_z = rem(z + 8 + jnp.where(rem(m, 2) == 1, -div(m + 1, 2), div(m, 2)), 8)
        return m, s, from_z

    def peer(along, d):
        return rem(y + along * d, 4) * 4 + rem(x + (1 - along) * d, 4)

    def place(along):
        return x * (1 - along) + y * along

    def multiply(u, s, from_leaf, e):
        along = rem(u, 2)
        block = blocks[block_table[s * 16 + from_leaf]]
        panel = panels[from_leaf, s].reshape(256, 256)
        product = jnp.dot(block, panel, preferred_element_type=F32).astype(BF16)
        for q in range(16):
            to = (q % 4) * (1 - along) + (q // 4) * along
            sub = (q // 4) * (1 - along) + (q % 4) * along
            products[u, to, div(sub, 2), e, rem(sub, 2)] = product[q * 16 : q * 16 + 16, :]

    def gather(u):
        m, s, from_z = place_of(u)
        held = panels.at[2 * from_z + core, s]
        pl.when(m == 0)(lambda: wait(held, p2_recv.at[s]))
        for h in range(2):
            half = held.at[pl.ds(h * 8, 8)]
            pl.when(m > 0)(lambda: wait(half, ring_recv.at[m * 4 + s * 2 + h]))
            up = (m == 0) | ((rem(m, 2) == 1) & (m <= (5 if h == 0 else 3)))
            down = (m == 0) | ((rem(m, 2) == 0) & (m <= (4 if h == 0 else 6)))

            @pl.when(up)
            def _():
                slot = jnp.where(m == 0, 1, m + 2)
                send(half, half, ring_send, ring_recv.at[slot * 4 + s * 2 + h], rem(z + 1, 8) * 2 + core, grp)

            @pl.when(down)
            def _():
                slot = jnp.where(m == 0, 2, jnp.minimum(m + 2, 7))
                send(half, half, ring_send, ring_recv.at[slot * 4 + s * 2 + h], rem(z + 7, 8) * 2 + core, grp)

        send(held, held, sib_send, sib_recv.at[u], 2 * z + 1 - core, grp)
        multiply(u, s, 2 * from_z + core, 0)

    def is_direct(u):
        return u >= DIRECT

    def multiply_other(u):
        m, s, from_z = place_of(u)
        from_leaf = 2 * from_z + 1 - core
        wait(panels.at[from_leaf, s], sib_recv.at[u])
        multiply(u, s, from_leaf, 1)
        along = rem(u, 2)
        opposite = rem(place(along) + 2, 4)

        @pl.when(~is_direct(u))
        def _():
            send(products.at[u, opposite, 0], halves.at[u, 0], half_send, half_recv.at[u], leaf, peer(along, 1))
            send(products.at[u, opposite, 1], halves.at[u, 1], half_send, half_recv.at[u], leaf, peer(along, 3))

        @pl.when(is_direct(u))
        def _():
            for d, slot in ((2, 2), (1, 0), (3, 1)):
                to = rem(place(along) + d, 4)
                send(products.at[u, to], sums.at[u, slot], sum_send, sum_recv.at[u], leaf, peer(along, d))

    def add_halves(u):
        along = rem(u, 2)
        after, before = rem(place(along) + 1, 4), rem(place(along) + 3, 4)
        wait(halves.at[u], half_recv.at[u])
        products[u, after, 0] = (products[u, after, 0].astype(F32) + halves[u, 0].astype(F32)).astype(BF16)
        send(products.at[u, after], sums.at[u, 0], sum_send_two, sum_recv.at[u], leaf, peer(along, 1))
        products[u, before, 1] = (products[u, before, 1].astype(F32) + halves[u, 1].astype(F32)).astype(BF16)
        send(products.at[u, before], sums.at[u, 1], sum_send_two, sum_recv.at[u], leaf, peer(along, 3))

    def add_sums(u, received):
        along = rem(u, 2)
        wait(sums.at[u, pl.ds(0, received)], sum_recv.at[u])
        total = products[u, place(along)].astype(F32)
        for slot in range(received):
            total = total + sums[u, slot].astype(F32)
        total = total.astype(BF16)
        for to in range(4):
            for e in range(2):
                parts[u, to, e] = total[to // 2, e, to % 2]
        for d in (2, 1, 3):
            to = rem(place(1 - along) + d, 4)
            send(parts.at[u, to], parts_in.at[u, d - 1], part_send, part_recv.at[u], leaf, peer(1 - along, d))

    def add_parts(u):
        m, s, from_z = place_of(u)
        wait(parts_in.at[u], part_recv.at[u])
        total = parts[u, place(1 - rem(u, 2))].astype(F32)
        for d in range(3):
            total = total + parts_in[u, d].astype(F32)
        finals[u] = (-total).astype(BF16)

        def send_rows(s):
            @pl.when(m == 0)
            def _():
                pltpu.make_async_copy(finals.at[u, 0], rows[s].at[leaf], row_recv.at[s]).start()

            @pl.when(m > 0)
            def _():
                send(finals.at[u, 0], rows[s].at[leaf], row_send, row_recv.at[s], 2 * from_z + core, grp)

            send(finals.at[u, 1], rows[s].at[leaf], row_send, row_recv.at[s], 2 * from_z + 1 - core, grp)

        pl.when(s == 0)(lambda: send_rows(0))
        pl.when(s == 1)(lambda: send_rows(1))

    def step(t, carry):
        both = range(2)

        @pl.when(t < 8)
        def _():
            for i in both:
                gather(2 * t + i)
            for i in both:
                multiply_other(2 * t + i)

        @pl.when((t >= LAG_HALVES) & (t < 8 + LAG_HALVES))
        def _():
            for i in both:
                u = 2 * (t - LAG_HALVES) + i
                pl.when(~is_direct(u))(lambda: add_halves(u))

        @pl.when((t >= LAG_SUMS) & (t < 8 + LAG_SUMS))
        def _():
            for i in both:
                u = 2 * (t - LAG_SUMS) + i
                pl.when(~is_direct(u))(lambda: add_sums(u, 2))
                pl.when(is_direct(u))(lambda: add_sums(u, 3))

        @pl.when(t >= LAG_PARTS)
        def _():
            for i in both:
                add_parts(2 * (t - LAG_PARTS) + i)

        return carry

    lax.fori_loop(0, 8 + LAG_PARTS, step, 0)

    def send_end(kind, s):
        sem = end_recv.at[kind * (1 + s)]
        for to in peers:
            send(leaving.at[kind, s, to], arriving.at[kind, s, grp], end_send, sem, leaf, to)
        pltpu.make_async_copy(leaving.at[kind, s, grp], arriving.at[kind, s, grp], sem).start()

    def diag_part(s):
        value = lax.dot_general(
            slices[s][...].reshape(256, 256), leaving[0, s].reshape(256, 256), (((0,), (0,)), ((), ())),
            preferred_element_type=F32,
        )
        leaving[1, s] = value.astype(BF16).reshape(16, 16, 256)
        send_end(1, s)

    for s in range(2):
        wait(rows[s], row_recv.at[s])
        for j in range(16):
            leaving[0, s, j] = rows[s][own_table[s * 16 + j]]
        send_end(0, s)
    for s in range(2):
        diag_part(s)

    wait(diag_inverse, table_sem.at[2])
    wait(arriving.at[0], end_recv.at[0])
    off_out[...] = arriving[0]
    for s in range(2):
        wait(arriving.at[1, s], end_recv.at[1 + s])
        total = arriving[1, s, 0].astype(F32)
        for g in range(1, 16):
            total = total + arriving[1, s, g].astype(F32)
        diag_out[s] = diag_inverse[s] - total

    for s in range(2):
        wait(slices[s].at[pl.ds(0, 15)], p1_send.at[s])
        wait(stage.at[s, pl.ds(0, 15)], p2_send.at[s])
    wait(leaving.at[:, :, pl.ds(0, 15)], end_send)
    wait(panels.at[pl.ds(0, 7)], ring_send)
    wait(panels.at[pl.ds(0, 8)], sib_send)
    wait(halves.at[pl.ds(0, DIRECT)], half_send)
    wait(sums.at[pl.ds(0, DIRECT), pl.ds(0, 2)], sum_send_two)
    wait(sums.at[pl.ds(0, 16 - DIRECT)], sum_send)
    wait(parts_in, part_send)
    wait(finals.at[pl.ds(0, 15)], row_send)


def finish(off, diag, off_out, diag_out):
    off_out[...] = off[...]
    diag_out[...] = diag[...]


def per_device(kept_inverse, owner_map, structure, l_panel, diag_inverse):
    hbm = pl.BlockSpec(memory_space=pl.ANY)
    vmem = pl.BlockSpec(memory_space=pltpu.VMEM)
    dma = pltpu.SemaphoreType.DMA
    off, diag = pl.pallas_call(
        kernel,
        out_shape=(
            jax.ShapeDtypeStruct((2, 16, 16, 256), BF16),
            jax.ShapeDtypeStruct((2, 16, 256), F32),
        ),
        in_specs=[hbm] * 5,
        out_specs=(vmem, vmem),
        scratch_shapes=[
            pltpu.VMEM((16, 256, 256), BF16),
            pltpu.VMEM((16, 16, 256), BF16),
            pltpu.VMEM((16, 16, 256), BF16),
            pltpu.VMEM((2, 16, 16, 256), BF16),
            pltpu.VMEM((16, 2, 16, 16, 256), BF16),
            pltpu.VMEM((16, 4, 2, 2, 2, 16, 256), BF16),
            pltpu.VMEM((16, 2, 2, 2, 16, 256), BF16),
            pltpu.VMEM((16, 3, 2, 2, 2, 16, 256), BF16),
            pltpu.VMEM((16, 4, 2, 16, 256), BF16),
            pltpu.VMEM((16, 3, 2, 16, 256), BF16),
            pltpu.VMEM((16, 2, 16, 256), BF16),
            pltpu.VMEM((16, 16, 256), BF16),
            pltpu.VMEM((16, 16, 256), BF16),
            pltpu.VMEM((2, 2, 16, 16, 256), BF16),
            pltpu.VMEM((2, 2, 16, 16, 256), BF16),
            pltpu.VMEM((2, 256, 256), BF16),
            pltpu.VMEM((2, 16, 256), F32),
            pltpu.SMEM((64,), jnp.int32),
            pltpu.SMEM((2, 16, 16), jnp.int32),
            pltpu.SMEM((32,), jnp.int32),
            pltpu.SMEM((32,), jnp.int32),
            pltpu.SMEM((32,), jnp.int32),
            dma, dma((4,)), dma((2,)), dma((2,)), dma((2,)), dma((2,)),
            dma, dma((32,)), dma, dma((16,)),
            dma, dma((16,)), dma, dma, dma((16,)), dma, dma((16,)),
            dma, dma((2,)), dma, dma((3,)),
        ],
        compiler_params=pltpu.CompilerParams(
            collective_id=0, has_side_effects=True, vmem_limit_bytes=VMEM_LIMIT
        ),
    )(owner_map, structure, kept_inverse, l_panel, diag_inverse)
    off, diag = pl.pallas_call(
        finish,
        out_shape=(jax.ShapeDtypeStruct(off.shape, off.dtype), jax.ShapeDtypeStruct(diag.shape, diag.dtype)),
        in_specs=[vmem, vmem],
        out_specs=(vmem, vmem),
    )(off, diag)
    return off.reshape(2, 256, 256), diag


def solution(mesh):
    in_specs = (
        P("leaf", "grp"),
        P(),
        P(),
        P(None, ("leaf", "grp"), None),
        P(None, ("leaf", "grp"), None),
    )
    out_specs = (P(None, ("leaf", "grp"), None), P(None, ("leaf", "grp"), None))
    return jax.shard_map(
        per_device, mesh=mesh, in_specs=in_specs, out_specs=out_specs, check_vma=False
    )
```

```python
import jax
import jax.numpy as jnp
from jax import lax
from jax.experimental import pallas as pl
from jax.experimental.pallas import tpu as pltpu
from jax.sharding import PartitionSpec as P

MESH = pl.DeviceIdType.MESH
F32 = jnp.float32
BF16 = jnp.bfloat16
VMEM_LIMIT = 60 * 1024 * 1024
LAG_HALVES, LAG_SUMS, LAG_PARTS = 1, 3, 6
DIRECT = 14
FARTHEST_FIRST = sorted(
    ((dy, dx) for dy in range(4) for dx in range(4) if dy or dx), key=lambda d: -(min(d[0], 4 - d[0]) + min(d[1], 4 - d[1]))
)


def rem(a, n):
    return lax.rem(a, jnp.int32(n))


def div(a, n):
    return lax.div(a, jnp.int32(n))


def kernel(
    owner_hbm, structure_hbm, stored, l_panel_hbm, diag_hbm,
    off_out, diag_out,
    blocks, slices_0, slices_1, stage, panels, products, halves, sums, parts, parts_in, finals, rows_0, rows_1, leaving, arriving,
    l_panel, diag_inverse, owner, structure, own_table, k_table, block_table,
    in_sem, table_sem, p1_send, p1_recv, p2_send, p2_recv, ring_send, ring_recv, sib_send, sib_recv,
    half_send, half_recv, sum_send_two, sum_send, sum_recv, part_send, part_recv, row_send, row_recv,
    end_send, end_recv,
):
    slices, rows = (slices_0, slices_1), (rows_0, rows_1)
    leaf = lax.axis_index("leaf")
    grp = lax.axis_index("grp")
    z, core = div(leaf, 2), rem(leaf, 2)
    y, x = div(grp, 4), rem(grp, 4)

    def send(src, dst, send_sem, recv_sem, to_leaf, to_grp):
        pltpu.make_async_remote_copy(
            src_ref=src, dst_ref=dst, send_sem=send_sem, recv_sem=recv_sem,
            device_id=(to_leaf, to_grp), device_id_type=MESH,
        ).start()

    def wait(ref, sem):
        pltpu.make_async_copy(ref, ref, sem).wait()

    barrier = pltpu.get_barrier_semaphore()
    pltpu.make_async_copy(l_panel_hbm, l_panel, table_sem.at[3]).start()
    peers = [rem(y + dy, 4) * 4 + rem(x + dx, 4) for dy, dx in FARTHEST_FIRST]
    for to in peers:
        pl.semaphore_signal(barrier, inc=1, device_id=(leaf, to), device_id_type=MESH)

    def greet(d, carry):
        pl.semaphore_signal(barrier, inc=1, device_id=(rem(leaf + d, 16), grp), device_id_type=MESH)
        return carry

    lax.fori_loop(1, 16, greet, 0)
    pltpu.make_async_copy(owner_hbm, owner, table_sem.at[0]).start()
    pltpu.make_async_copy(structure_hbm, structure, table_sem.at[1]).start()
    pltpu.make_async_copy(diag_hbm, diag_inverse, table_sem.at[2]).start()
    for a in range(4):
        for b in range(4):
            pltpu.make_async_copy(
                stored.at[pl.ds(a * 256, 256), pl.ds(b * 256, 256)], blocks.at[a * 4 + b], in_sem
            ).start()
    wait(l_panel, table_sem.at[3])
    pl.semaphore_wait(barrier, 30)

    def rows_of(r):
        return pl.ds(pl.multiple_of(r * 16, 16), 16)

    def send_slices(s):
        for to in peers:
            send(l_panel.at[s, rows_of(to), :], slices[s].at[grp], p1_send.at[s], p1_recv.at[s], leaf, to)
        pltpu.make_async_copy(l_panel.at[s, rows_of(grp), :], slices[s].at[grp], p1_recv.at[s]).start()

    send_slices(0)

    wait(owner, table_sem.at[0])
    wait(structure, table_sem.at[1])
    for s in range(2):
        for j in range(16):
            own_table[s * 16 + j] = owner[structure[s, leaf, j]] >> 2

    def find_k(q, carry):
        for s in range(2):
            k = jnp.int32(0)
            for j in range(16):
                k = jnp.where(own_table[s * 16 + j] == q, j, k)
            k_table[s * 16 + q] = k
        return carry

    lax.fori_loop(0, 16, find_k, 0)
    send_slices(1)

    def find_block(i, carry):
        for s in range(2):
            row, col = jnp.int32(0), jnp.int32(0)
            for j in range(16):
                slot = owner[structure[s, i, j]]
                held_by, pick = slot >> 2, slot & 3
                row = jnp.where(held_by == leaf, pick, row)
                col = jnp.where(held_by == grp, pick, col)
            block_table[s * 16 + i] = row * 4 + col
        return carry

    for s in range(2):
        wait(slices[s], p1_recv.at[s])
        for q in range(16):
            stage[s, q] = slices[s][k_table[s * 16 + q]]
        for to in peers:
            send(stage.at[s, to], panels.at[leaf, s, grp], p2_send.at[s], p2_recv.at[s], leaf, to)
        pltpu.make_async_copy(stage.at[s, grp], panels.at[leaf, s, grp], p2_recv.at[s]).start()

    lax.fori_loop(0, 16, find_block, 0)
    wait(blocks, in_sem)

    def place_of(u):
        pair, turn = div(u + 2, 4), rem(u + 2, 4)
        m = jnp.where(u < 2, 0, jnp.where(u < 14, 2 * pair - 1 + rem(turn, 2), 7))
        s = jnp.where(u < 2, u, jnp.where(u < 14, div(turn, 2), u - 14))
        from_z = rem(z + 8 + jnp.where(rem(m, 2) == 1, -div(m + 1, 2), div(m, 2)), 8)
        return m, s, from_z

    def peer(along, d):
        return rem(y + along * d, 4) * 4 + rem(x + (1 - along) * d, 4)

    def place(along):
        return x * (1 - along) + y * along

    def multiply(u, s, from_leaf, e):
        along = rem(u, 2)
        block = blocks[block_table[s * 16 + from_leaf]]
        panel = panels[from_leaf, s].reshape(256, 256)
        product = jnp.dot(block, panel, preferred_element_type=F32).astype(BF16)
        for q in range(16):
            to = (q % 4) * (1 - along) + (q // 4) * along
            sub = (q // 4) * (1 - along) + (q % 4) * along
            products[u, to, div(sub, 2), e, rem(sub, 2)] = product[q * 16 : q * 16 + 16, :]

    def gather(u, h):
        m, s, from_z = place_of(u)
        held = panels.at[2 * from_z + core, s]
        if h == 0:
            pl.when(m == 0)(lambda: wait(held, p2_recv.at[s]))
        half = held.at[pl.ds(h * 8, 8)]
        pl.when(m > 0)(lambda: wait(half, ring_recv.at[m * 4 + s * 2 + h]))
        up = (m == 0) | ((rem(m, 2) == 1) & (m <= (5 if h == 0 else 3)))
        down = (m == 0) | ((rem(m, 2) == 0) & (m <= (4 if h == 0 else 6)))

        @pl.when(up)
        def _():
            slot = jnp.where(m == 0, 1, m + 2)
            send(half, half, ring_send, ring_recv.at[slot * 4 + s * 2 + h], rem(z + 1, 8) * 2 + core, grp)

        @pl.when(down)
        def _():
            slot = jnp.where(m == 0, 2, jnp.minimum(m + 2, 7))
            send(half, half, ring_send, ring_recv.at[slot * 4 + s * 2 + h], rem(z + 7, 8) * 2 + core, grp)

        send(half, half, sib_send, sib_recv.at[u], 2 * z + 1 - core, grp)

    def multiply_own(u):
        m, s, from_z = place_of(u)
        multiply(u, s, 2 * from_z + core, 0)

    def is_direct(u):
        return u >= DIRECT

    def multiply_other(u):
        m, s, from_z = place_of(u)
        from_leaf = 2 * from_z + 1 - core
        wait(panels.at[from_leaf, s], sib_recv.at[u])
        multiply(u, s, from_leaf, 1)
        along = rem(u, 2)
        opposite = rem(place(along) + 2, 4)

        @pl.when(~is_direct(u))
        def _():
            send(products.at[u, opposite, 0], halves.at[u, 0], half_send, half_recv.at[u], leaf, peer(along, 1))
            send(products.at[u, opposite, 1], halves.at[u, 1], half_send, half_recv.at[u], leaf, peer(along, 3))

        @pl.when(is_direct(u))
        def _():
            for d, slot in ((2, 2), (1, 0), (3, 1)):
                to = rem(place(along) + d, 4)
                send(products.at[u, to], sums.at[u, slot], sum_send, sum_recv.at[u], leaf, peer(along, d))

    def add_halves(u):
        along = rem(u, 2)
        after, before = rem(place(along) + 1, 4), rem(place(along) + 3, 4)
        wait(halves.at[u], half_recv.at[u])
        products[u, after, 0] = (products[u, after, 0].astype(F32) + halves[u, 0].astype(F32)).astype(BF16)
        send(products.at[u, after], sums.at[u, 0], sum_send_two, sum_recv.at[u], leaf, peer(along, 1))
        products[u, before, 1] = (products[u, before, 1].astype(F32) + halves[u, 1].astype(F32)).astype(BF16)
        send(products.at[u, before], sums.at[u, 1], sum_send_two, sum_recv.at[u], leaf, peer(along, 3))

    def add_sums(u, received):
        along = rem(u, 2)
        wait(sums.at[u, pl.ds(0, received)], sum_recv.at[u])
        total = products[u, place(along)].astype(F32)
        for slot in range(received):
            total = total + sums[u, slot].astype(F32)
        total = total.astype(BF16)
        for to in range(4):
            for e in range(2):
                parts[u, to, e] = total[to // 2, e, to % 2]
        for d in (2, 1, 3):
            to = rem(place(1 - along) + d, 4)
            send(parts.at[u, to], parts_in.at[u, d - 1], part_send, part_recv.at[u], leaf, peer(1 - along, d))

    def add_parts(u):
        m, s, from_z = place_of(u)
        wait(parts_in.at[u], part_recv.at[u])
        total = parts[u, place(1 - rem(u, 2))].astype(F32)
        for d in range(3):
            total = total + parts_in[u, d].astype(F32)
        finals[u] = (-total).astype(BF16)

        def send_rows(s):
            @pl.when(m == 0)
            def _():
                pltpu.make_async_copy(finals.at[u, 0], rows[s].at[leaf], row_recv.at[s]).start()

            @pl.when(m > 0)
            def _():
                send(finals.at[u, 0], rows[s].at[leaf], row_send, row_recv.at[s], 2 * from_z + core, grp)

            send(finals.at[u, 1], rows[s].at[leaf], row_send, row_recv.at[s], 2 * from_z + 1 - core, grp)

        pl.when(s == 0)(lambda: send_rows(0))
        pl.when(s == 1)(lambda: send_rows(1))

    def step(t, carry):
        both = range(2)

        @pl.when(t < 8)
        def _():
            for i in both:
                for h in both:
                    gather(2 * t + i, h)
                multiply_own(2 * t + i)
            for i in both:
                multiply_other(2 * t + i)

        def halves_stage():
            @pl.when((t >= LAG_HALVES) & (t < 8 + LAG_HALVES))
            def _():
                for i in both:
                    u = 2 * (t - LAG_HALVES) + i
                    pl.when(~is_direct(u))(lambda: add_halves(u))

        def sums_stage():
            @pl.when((t >= LAG_SUMS) & (t < 8 + LAG_SUMS))
            def _():
                for i in both:
                    pair = t - LAG_SUMS
                    pair = jnp.where(pair == 6, 7, jnp.where(pair == 7, 6, pair))
                    u = 2 * pair + i
                    pl.when(~is_direct(u))(lambda: add_sums(u, 2))
                    pl.when(is_direct(u))(lambda: add_sums(u, 3))

        def parts_stage():
            @pl.when(t >= LAG_PARTS)
            def _():
                for i in both:
                    u = 2 * (t - LAG_PARTS) + i
                    u = jnp.where(u == 12, 14, jnp.where((u == 13) | (u == 14), u - 1, u))
                    add_parts(u)

        sums_stage()
        halves_stage()
        parts_stage()

        return carry

    lax.fori_loop(0, 8 + LAG_PARTS, step, 0)

    def send_end(kind, s):
        sem = end_recv.at[kind * (1 + s)]
        for to in peers:
            send(leaving.at[kind, s, to], arriving.at[kind, s, grp], end_send, sem, leaf, to)
        pltpu.make_async_copy(leaving.at[kind, s, grp], arriving.at[kind, s, grp], sem).start()

    def diag_part(s):
        value = lax.dot_general(
            slices[s][...].reshape(256, 256), leaving[0, s].reshape(256, 256), (((0,), (0,)), ((), ())),
            preferred_element_type=F32,
        )
        leaving[1, s] = value.astype(BF16).reshape(16, 16, 256)
        send_end(1, s)

    for s in range(2):
        wait(rows[s], row_recv.at[s])
        for j in range(16):
            leaving[0, s, j] = rows[s][own_table[s * 16 + j]]
        send_end(0, s)
        diag_part(s)

    wait(diag_inverse, table_sem.at[2])
    wait(arriving.at[0], end_recv.at[0])
    pltpu.make_async_copy(arriving.at[0], off_out, table_sem.at[0]).start()
    for s in range(2):
        wait(arriving.at[1, s], end_recv.at[1 + s])
        total = arriving[1, s, 0].astype(F32)
        for g in range(1, 16):
            total = total + arriving[1, s, g].astype(F32)
        diag_out[s] = diag_inverse[s] - total

    pltpu.make_async_copy(arriving.at[0], off_out, table_sem.at[0]).wait()

    for s in range(2):
        wait(slices[s].at[pl.ds(0, 15)], p1_send.at[s])
        wait(stage.at[s, pl.ds(0, 15)], p2_send.at[s])
    wait(leaving.at[:, :, pl.ds(0, 15)], end_send)
    wait(panels.at[pl.ds(0, 7)], ring_send)
    wait(panels.at[pl.ds(0, 8)], sib_send)
    wait(halves.at[pl.ds(0, DIRECT)], half_send)
    wait(sums.at[pl.ds(0, DIRECT), pl.ds(0, 2)], sum_send_two)
    wait(sums.at[pl.ds(0, 16 - DIRECT)], sum_send)
    wait(parts_in, part_send)
    wait(finals.at[pl.ds(0, 15)], row_send)


def finish(off, diag, off_out, diag_out):
    off_out[...] = off[...]
    diag_out[...] = diag[...]


def per_device(kept_inverse, owner_map, structure, l_panel, diag_inverse):
    hbm = pl.BlockSpec(memory_space=pl.ANY)
    vmem = pl.BlockSpec(memory_space=pltpu.VMEM)
    dma = pltpu.SemaphoreType.DMA
    off, diag = pl.pallas_call(
        kernel,
        out_shape=(
            jax.ShapeDtypeStruct((2, 16, 16, 256), BF16),
            jax.ShapeDtypeStruct((2, 16, 256), F32),
        ),
        in_specs=[hbm] * 5,
        out_specs=(hbm, vmem),
        scratch_shapes=[
            pltpu.VMEM((16, 256, 256), BF16),
            pltpu.VMEM((16, 16, 256), BF16),
            pltpu.VMEM((16, 16, 256), BF16),
            pltpu.VMEM((2, 16, 16, 256), BF16),
            pltpu.VMEM((16, 2, 16, 16, 256), BF16),
            pltpu.VMEM((16, 4, 2, 2, 2, 16, 256), BF16),
            pltpu.VMEM((16, 2, 2, 2, 16, 256), BF16),
            pltpu.VMEM((16, 3, 2, 2, 2, 16, 256), BF16),
            pltpu.VMEM((16, 4, 2, 16, 256), BF16),
            pltpu.VMEM((16, 3, 2, 16, 256), BF16),
            pltpu.VMEM((16, 2, 16, 256), BF16),
            pltpu.VMEM((16, 16, 256), BF16),
            pltpu.VMEM((16, 16, 256), BF16),
            pltpu.VMEM((2, 2, 16, 16, 256), BF16),
            pltpu.VMEM((2, 2, 16, 16, 256), BF16),
            pltpu.VMEM((2, 256, 256), BF16),
            pltpu.VMEM((2, 16, 256), F32),
            pltpu.SMEM((64,), jnp.int32),
            pltpu.SMEM((2, 16, 16), jnp.int32),
            pltpu.SMEM((32,), jnp.int32),
            pltpu.SMEM((32,), jnp.int32),
            pltpu.SMEM((32,), jnp.int32),
            dma, dma((4,)), dma((2,)), dma((2,)), dma((2,)), dma((2,)),
            dma, dma((32,)), dma, dma((16,)),
            dma, dma((16,)), dma, dma, dma((16,)), dma, dma((16,)),
            dma, dma((2,)), dma, dma((3,)),
        ],
        compiler_params=pltpu.CompilerParams(
            collective_id=0, has_side_effects=True, vmem_limit_bytes=VMEM_LIMIT
        ),
    )(owner_map, structure, kept_inverse, l_panel, diag_inverse)
    shapes = (jax.ShapeDtypeStruct(off.shape, off.dtype), jax.ShapeDtypeStruct(diag.shape, diag.dtype))
    off, diag = pl.pallas_call(
        finish, out_shape=shapes, in_specs=[vmem, vmem], out_specs=(vmem, vmem)
    )(off, diag)
    return off.reshape(2, 256, 256), diag


def solution(mesh):
    in_specs = (
        P("leaf", "grp"),
        P(),
        P(),
        P(None, ("leaf", "grp"), None),
        P(None, ("leaf", "grp"), None),
    )
    out_specs = (P(None, ("leaf", "grp"), None), P(None, ("leaf", "grp"), None))
    return jax.shard_map(
        per_device, mesh=mesh, in_specs=in_specs, out_specs=out_specs, check_vma=False
    )
```

```python
import jax
import jax.numpy as jnp
from jax import lax
from jax.experimental import pallas as pl
from jax.experimental.pallas import tpu as pltpu
from jax.sharding import PartitionSpec as P

MESH = pl.DeviceIdType.MESH
F32 = jnp.float32
BF16 = jnp.bfloat16
VMEM_LIMIT = 60 * 1024 * 1024
LAG_HALVES, LAG_SUMS, LAG_PARTS = 1, 3, 6
DIRECT = 14
FARTHEST_FIRST = sorted(
    ((dy, dx) for dy in range(4) for dx in range(4) if dy or dx), key=lambda d: -(min(d[0], 4 - d[0]) + min(d[1], 4 - d[1]))
)


def rem(a, n):
    return lax.rem(a, jnp.int32(n))


def div(a, n):
    return lax.div(a, jnp.int32(n))


def kernel(
    owner_hbm, structure_hbm, stored, l_panel_hbm, diag_hbm,
    off_out, diag_out,
    blocks, slices_0, slices_1, stage, panels, products, halves, sums, parts, parts_in, finals, rows_0, rows_1, leaving, arriving,
    l_panel, diag_inverse, owner, structure, own_table, k_table, block_table,
    in_sem, table_sem, p1_send, p1_recv, p2_send, p2_recv, ring_send, ring_recv, sib_send, sib_recv,
    half_send, half_recv, sum_send_two, sum_send, sum_recv, part_send, part_recv, row_send, row_recv,
    end_send, end_recv,
):
    slices, rows = (slices_0, slices_1), (rows_0, rows_1)
    leaf = lax.axis_index("leaf")
    grp = lax.axis_index("grp")
    z, core = div(leaf, 2), rem(leaf, 2)
    y, x = div(grp, 4), rem(grp, 4)

    def send(src, dst, send_sem, recv_sem, to_leaf, to_grp):
        pltpu.make_async_remote_copy(
            src_ref=src, dst_ref=dst, send_sem=send_sem, recv_sem=recv_sem,
            device_id=(to_leaf, to_grp), device_id_type=MESH,
        ).start()

    def wait(ref, sem):
        pltpu.make_async_copy(ref, ref, sem).wait()

    barrier = pltpu.get_barrier_semaphore()
    pltpu.make_async_copy(l_panel_hbm, l_panel, table_sem.at[3]).start()
    peers = [rem(y + dy, 4) * 4 + rem(x + dx, 4) for dy, dx in FARTHEST_FIRST]
    for to in peers:
        pl.semaphore_signal(barrier, inc=1, device_id=(leaf, to), device_id_type=MESH)

    def greet(d, carry):
        pl.semaphore_signal(barrier, inc=1, device_id=(rem(leaf + d, 16), grp), device_id_type=MESH)
        return carry

    lax.fori_loop(1, 16, greet, 0)
    pltpu.make_async_copy(owner_hbm, owner, table_sem.at[0]).start()
    pltpu.make_async_copy(structure_hbm, structure, table_sem.at[1]).start()
    pltpu.make_async_copy(diag_hbm, diag_inverse, table_sem.at[2]).start()
    for a in range(4):
        for b in range(4):
            pltpu.make_async_copy(
                stored.at[pl.ds(a * 256, 256), pl.ds(b * 256, 256)], blocks.at[a * 4 + b], in_sem
            ).start()
    wait(l_panel, table_sem.at[3])
    pl.semaphore_wait(barrier, 30)

    def rows_of(r):
        return pl.ds(pl.multiple_of(r * 16, 16), 16)

    def send_slices(s):
        for to in peers:
            send(l_panel.at[s, rows_of(to), :], slices[s].at[grp], p1_send.at[s], p1_recv.at[s], leaf, to)
        pltpu.make_async_copy(l_panel.at[s, rows_of(grp), :], slices[s].at[grp], p1_recv.at[s]).start()

    send_slices(0)

    wait(owner, table_sem.at[0])
    wait(structure, table_sem.at[1])
    for s in range(2):
        for j in range(16):
            own_table[s * 16 + j] = owner[structure[s, leaf, j]] >> 2

    def find_k(q, carry):
        for s in range(2):
            k = jnp.int32(0)
            for j in range(16):
                k = jnp.where(own_table[s * 16 + j] == q, j, k)
            k_table[s * 16 + q] = k
        return carry

    lax.fori_loop(0, 16, find_k, 0)
    send_slices(1)

    def find_block(i, carry):
        for s in range(2):
            row, col = jnp.int32(0), jnp.int32(0)
            for j in range(16):
                slot = owner[structure[s, i, j]]
                held_by, pick = slot >> 2, slot & 3
                row = jnp.where(held_by == leaf, pick, row)
                col = jnp.where(held_by == grp, pick, col)
            block_table[s * 16 + i] = row * 4 + col
        return carry

    for s in range(2):
        wait(slices[s], p1_recv.at[s])
        for q in range(16):
            stage[s, q] = slices[s][k_table[s * 16 + q]]
        for to in peers:
            send(stage.at[s, to], panels.at[leaf, s, grp], p2_send.at[s], p2_recv.at[s], leaf, to)
        pltpu.make_async_copy(stage.at[s, grp], panels.at[leaf, s, grp], p2_recv.at[s]).start()

    lax.fori_loop(0, 16, find_block, 0)
    wait(blocks, in_sem)

    def place_of(u):
        pair, turn = div(u + 2, 4), rem(u + 2, 4)
        m = jnp.where(u < 2, 0, jnp.where(u < 14, 2 * pair - 1 + rem(turn, 2), 7))
        s = jnp.where(u < 2, u, jnp.where(u < 14, div(turn, 2), u - 14))
        from_z = rem(z + 8 + jnp.where(rem(m, 2) == 1, -div(m + 1, 2), div(m, 2)), 8)
        return m, s, from_z

    def peer(along, d):
        return rem(y + along * d, 4) * 4 + rem(x + (1 - along) * d, 4)

    def place(along):
        return x * (1 - along) + y * along

    def multiply(u, s, from_leaf, e):
        along = rem(u, 2)
        block = blocks[block_table[s * 16 + from_leaf]]
        panel = panels[from_leaf, s].reshape(256, 256)
        product = jnp.dot(block, panel, preferred_element_type=F32).astype(BF16)
        for q in range(16):
            to = (q % 4) * (1 - along) + (q // 4) * along
            sub = (q // 4) * (1 - along) + (q % 4) * along
            products[u, to, div(sub, 2), e, rem(sub, 2)] = product[q * 16 : q * 16 + 16, :]

    def gather(u, h):
        m, s, from_z = place_of(u)
        held = panels.at[2 * from_z + core, s]
        if h == 0:
            pl.when(m == 0)(lambda: wait(held, p2_recv.at[s]))
        half = held.at[pl.ds(h * 8, 8)]
        pl.when(m > 0)(lambda: wait(half, ring_recv.at[m * 4 + s * 2 + h]))
        up = (m == 0) | ((rem(m, 2) == 1) & (m <= (5 if h == 0 else 3)))
        down = (m == 0) | ((rem(m, 2) == 0) & (m <= (4 if h == 0 else 6)))

        @pl.when(up)
        def _():
            slot = jnp.where(m == 0, 1, m + 2)
            send(half, half, ring_send, ring_recv.at[slot * 4 + s * 2 + h], rem(z + 1, 8) * 2 + core, grp)

        @pl.when(down)
        def _():
            slot = jnp.where(m == 0, 2, jnp.minimum(m + 2, 7))
            send(half, half, ring_send, ring_recv.at[slot * 4 + s * 2 + h], rem(z + 7, 8) * 2 + core, grp)

        send(half, half, sib_send, sib_recv.at[u], 2 * z + 1 - core, grp)

    def multiply_own(u):
        m, s, from_z = place_of(u)
        multiply(u, s, 2 * from_z + core, 0)

    def is_direct(u):
        return u >= DIRECT

    def multiply_other(u):
        m, s, from_z = place_of(u)
        from_leaf = 2 * from_z + 1 - core
        wait(panels.at[from_leaf, s], sib_recv.at[u])
        multiply(u, s, from_leaf, 1)
        along = rem(u, 2)
        opposite = rem(place(along) + 2, 4)

        @pl.when(~is_direct(u))
        def _():
            send(products.at[u, opposite, 0], halves.at[u, 0], half_send, half_recv.at[u], leaf, peer(along, 1))
            send(products.at[u, opposite, 1], halves.at[u, 1], half_send, half_recv.at[u], leaf, peer(along, 3))

        @pl.when(is_direct(u))
        def _():
            for d, slot in ((2, 2), (1, 0), (3, 1)):
                to = rem(place(along) + d, 4)
                send(products.at[u, to], sums.at[u, slot], sum_send, sum_recv.at[u], leaf, peer(along, d))

    def add_halves(u):
        along = rem(u, 2)
        after, before = rem(place(along) + 1, 4), rem(place(along) + 3, 4)
        wait(halves.at[u], half_recv.at[u])
        products[u, after, 0] = (products[u, after, 0].astype(F32) + halves[u, 0].astype(F32)).astype(BF16)
        send(products.at[u, after], sums.at[u, 0], sum_send_two, sum_recv.at[u], leaf, peer(along, 1))
        products[u, before, 1] = (products[u, before, 1].astype(F32) + halves[u, 1].astype(F32)).astype(BF16)
        send(products.at[u, before], sums.at[u, 1], sum_send_two, sum_recv.at[u], leaf, peer(along, 3))

    def add_sums(u, received):
        along = rem(u, 2)
        wait(sums.at[u, pl.ds(0, received)], sum_recv.at[u])
        total = products[u, place(along)].astype(F32)
        for slot in range(received):
            total = total + sums[u, slot].astype(F32)
        total = total.astype(BF16)
        for to in range(4):
            for e in range(2):
                parts[u, to, e] = total[to // 2, e, to % 2]
        for d in (2, 1, 3):
            to = rem(place(1 - along) + d, 4)
            send(parts.at[u, to], parts_in.at[u, d - 1], part_send, part_recv.at[u], leaf, peer(1 - along, d))

    def add_parts(u):
        m, s, from_z = place_of(u)
        wait(parts_in.at[u], part_recv.at[u])
        total = parts[u, place(1 - rem(u, 2))].astype(F32)
        for d in range(3):
            total = total + parts_in[u, d].astype(F32)
        finals[u] = (-total).astype(BF16)

        def send_rows(s):
            @pl.when(m == 0)
            def _():
                pltpu.make_async_copy(finals.at[u, 0], rows[s].at[leaf], row_recv.at[s]).start()

            @pl.when(m > 0)
            def _():
                send(finals.at[u, 0], rows[s].at[leaf], row_send, row_recv.at[s], 2 * from_z + core, grp)

            send(finals.at[u, 1], rows[s].at[leaf], row_send, row_recv.at[s], 2 * from_z + 1 - core, grp)

        pl.when(s == 0)(lambda: send_rows(0))
        pl.when(s == 1)(lambda: send_rows(1))

    def step(t, carry):
        both = range(2)

        def halves_stage():
            @pl.when((t >= LAG_HALVES) & (t < 8 + LAG_HALVES))
            def _():
                for i in both:
                    u = 2 * (t - LAG_HALVES) + i
                    pl.when(~is_direct(u))(lambda: add_halves(u))

        def sums_stage():
            @pl.when((t >= LAG_SUMS) & (t < 8 + LAG_SUMS))
            def _():
                for i in both:
                    pair = t - LAG_SUMS
                    pair = jnp.where(pair == 6, 7, jnp.where(pair == 7, 6, pair))
                    u = 2 * pair + i
                    pl.when(~is_direct(u))(lambda: add_sums(u, 2))
                    pl.when(is_direct(u))(lambda: add_sums(u, 3))

        def parts_stage():
            @pl.when(t >= LAG_PARTS)
            def _():
                for i in both:
                    u = 2 * (t - LAG_PARTS) + i
                    u = jnp.where(u == 12, 14, jnp.where((u == 13) | (u == 14), u - 1, u))
                    add_parts(u)

        @pl.when(t < 8)
        def _():
            for i in both:
                for h in both:
                    gather(2 * t + i, h)
            for i in both:
                multiply_own(2 * t + i)
                multiply_other(2 * t + i)

        sums_stage()
        halves_stage()
        parts_stage()

        return carry

    lax.fori_loop(0, 8 + LAG_PARTS, step, 0)

    def send_end(kind, s):
        sem = end_recv.at[kind * (1 + s)]
        for to in peers:
            send(leaving.at[kind, s, to], arriving.at[kind, s, grp], end_send, sem, leaf, to)
        pltpu.make_async_copy(leaving.at[kind, s, grp], arriving.at[kind, s, grp], sem).start()

    def diag_part(s):
        value = lax.dot_general(
            slices[s][...].reshape(256, 256), leaving[0, s].reshape(256, 256), (((0,), (0,)), ((), ())),
            preferred_element_type=F32,
        )
        leaving[1, s] = value.astype(BF16).reshape(16, 16, 256)
        send_end(1, s)

    for s in range(2):
        wait(rows[s], row_recv.at[s])
        for j in range(16):
            leaving[0, s, j] = rows[s][own_table[s * 16 + j]]
        send_end(0, s)
        diag_part(s)

    wait(diag_inverse, table_sem.at[2])
    wait(arriving.at[0], end_recv.at[0])
    pltpu.make_async_copy(arriving.at[0], off_out, table_sem.at[0]).start()
    for s in range(2):
        wait(arriving.at[1, s], end_recv.at[1 + s])
        total = arriving[1, s, 0].astype(F32)
        for g in range(1, 16):
            total = total + arriving[1, s, g].astype(F32)
        diag_out[s] = diag_inverse[s] - total

    pltpu.make_async_copy(arriving.at[0], off_out, table_sem.at[0]).wait()

    for s in range(2):
        wait(slices[s].at[pl.ds(0, 15)], p1_send.at[s])
        wait(stage.at[s, pl.ds(0, 15)], p2_send.at[s])
    wait(leaving.at[:, :, pl.ds(0, 15)], end_send)
    wait(panels.at[pl.ds(0, 7)], ring_send)
    wait(panels.at[pl.ds(0, 8)], sib_send)
    wait(halves.at[pl.ds(0, DIRECT)], half_send)
    wait(sums.at[pl.ds(0, DIRECT), pl.ds(0, 2)], sum_send_two)
    wait(sums.at[pl.ds(0, 16 - DIRECT)], sum_send)
    wait(parts_in, part_send)
    wait(finals.at[pl.ds(0, 15)], row_send)


def finish(off, diag, off_out, diag_out):
    off_out[...] = off[...]
    diag_out[...] = diag[...]


def per_device(kept_inverse, owner_map, structure, l_panel, diag_inverse):
    hbm = pl.BlockSpec(memory_space=pl.ANY)
    vmem = pl.BlockSpec(memory_space=pltpu.VMEM)
    dma = pltpu.SemaphoreType.DMA
    off, diag = pl.pallas_call(
        kernel,
        out_shape=(
            jax.ShapeDtypeStruct((2, 16, 16, 256), BF16),
            jax.ShapeDtypeStruct((2, 16, 256), F32),
        ),
        in_specs=[hbm] * 5,
        out_specs=(hbm, vmem),
        scratch_shapes=[
            pltpu.VMEM((16, 256, 256), BF16),
            pltpu.VMEM((16, 16, 256), BF16),
            pltpu.VMEM((16, 16, 256), BF16),
            pltpu.VMEM((2, 16, 16, 256), BF16),
            pltpu.VMEM((16, 2, 16, 16, 256), BF16),
            pltpu.VMEM((16, 4, 2, 2, 2, 16, 256), BF16),
            pltpu.VMEM((16, 2, 2, 2, 16, 256), BF16),
            pltpu.VMEM((16, 3, 2, 2, 2, 16, 256), BF16),
            pltpu.VMEM((16, 4, 2, 16, 256), BF16),
            pltpu.VMEM((16, 3, 2, 16, 256), BF16),
            pltpu.VMEM((16, 2, 16, 256), BF16),
            pltpu.VMEM((16, 16, 256), BF16),
            pltpu.VMEM((16, 16, 256), BF16),
            pltpu.VMEM((2, 2, 16, 16, 256), BF16),
            pltpu.VMEM((2, 2, 16, 16, 256), BF16),
            pltpu.VMEM((2, 256, 256), BF16),
            pltpu.VMEM((2, 16, 256), F32),
            pltpu.SMEM((64,), jnp.int32),
            pltpu.SMEM((2, 16, 16), jnp.int32),
            pltpu.SMEM((32,), jnp.int32),
            pltpu.SMEM((32,), jnp.int32),
            pltpu.SMEM((32,), jnp.int32),
            dma, dma((4,)), dma((2,)), dma((2,)), dma((2,)), dma((2,)),
            dma, dma((32,)), dma, dma((16,)),
            dma, dma((16,)), dma, dma, dma((16,)), dma, dma((16,)),
            dma, dma((2,)), dma, dma((3,)),
        ],
        compiler_params=pltpu.CompilerParams(
            collective_id=0, has_side_effects=True, vmem_limit_bytes=VMEM_LIMIT
        ),
    )(owner_map, structure, kept_inverse, l_panel, diag_inverse)
    shapes = (jax.ShapeDtypeStruct(off.shape, off.dtype), jax.ShapeDtypeStruct(diag.shape, diag.dtype))
    off, diag = pl.pallas_call(
        finish, out_shape=shapes, in_specs=[vmem, vmem], out_specs=(vmem, vmem)
    )(off, diag)
    return off.reshape(2, 256, 256), diag


def solution(mesh):
    in_specs = (
        P("leaf", "grp"),
        P(),
        P(),
        P(None, ("leaf", "grp"), None),
        P(None, ("leaf", "grp"), None),
    )
    out_specs = (P(None, ("leaf", "grp"), None), P(None, ("leaf", "grp"), None))
    return jax.shard_map(
        per_device, mesh=mesh, in_specs=in_specs, out_specs=out_specs, check_vma=False
    )
```

```python
import jax
import jax.numpy as jnp
from jax import lax
from jax.experimental import pallas as pl
from jax.experimental.pallas import tpu as pltpu
from jax.sharding import PartitionSpec as P

MESH = pl.DeviceIdType.MESH
F32 = jnp.float32
BF16 = jnp.bfloat16
VMEM_LIMIT = 60 * 1024 * 1024
LAG_HALVES, LAG_SUMS, LAG_PARTS = 1, 3, 6
EARLY = 4
DIRECT = 14
FARTHEST_FIRST = sorted(
    ((dy, dx) for dy in range(4) for dx in range(4) if dy or dx), key=lambda d: -(min(d[0], 4 - d[0]) + min(d[1], 4 - d[1]))
)


def rem(a, n):
    return lax.rem(a, jnp.int32(n))


def div(a, n):
    return lax.div(a, jnp.int32(n))


def kernel(
    owner_hbm, structure_hbm, stored, l_panel_hbm, diag_hbm,
    off_out, diag_out,
    blocks, slices_0, slices_1, stage, panels, products, halves, sums, parts, parts_in, finals, rows_0, rows_1, leaving, arriving,
    l_panel, diag_inverse, owner, structure, own_table, k_table, block_table,
    in_sem, table_sem, p1_send, p1_recv, p2_send, p2_recv, ring_send, ring_recv, sib_send, sib_recv,
    half_send, half_recv, sum_send_two, sum_send, sum_recv, part_send, part_recv, row_send, row_recv,
    end_send, end_recv,
):
    slices, rows = (slices_0, slices_1), (rows_0, rows_1)
    leaf = lax.axis_index("leaf")
    grp = lax.axis_index("grp")
    z, core = div(leaf, 2), rem(leaf, 2)
    y, x = div(grp, 4), rem(grp, 4)

    def send(src, dst, send_sem, recv_sem, to_leaf, to_grp):
        pltpu.make_async_remote_copy(
            src_ref=src, dst_ref=dst, send_sem=send_sem, recv_sem=recv_sem,
            device_id=(to_leaf, to_grp), device_id_type=MESH,
        ).start()

    def wait(ref, sem):
        pltpu.make_async_copy(ref, ref, sem).wait()

    barrier = pltpu.get_barrier_semaphore()
    pltpu.make_async_copy(l_panel_hbm, l_panel, table_sem.at[3]).start()
    peers = [rem(y + dy, 4) * 4 + rem(x + dx, 4) for dy, dx in FARTHEST_FIRST]
    for to in peers:
        pl.semaphore_signal(barrier, inc=1, device_id=(leaf, to), device_id_type=MESH)

    def greet(d, carry):
        pl.semaphore_signal(barrier, inc=1, device_id=(rem(leaf + d, 16), grp), device_id_type=MESH)
        return carry

    lax.fori_loop(1, 16, greet, 0)
    pltpu.make_async_copy(owner_hbm, owner, table_sem.at[0]).start()
    pltpu.make_async_copy(structure_hbm, structure, table_sem.at[1]).start()
    pltpu.make_async_copy(diag_hbm, diag_inverse, table_sem.at[2]).start()
    for a in range(4):
        for b in range(4):
            pltpu.make_async_copy(
                stored.at[pl.ds(a * 256, 256), pl.ds(b * 256, 256)], blocks.at[a * 4 + b], in_sem
            ).start()
    wait(l_panel, table_sem.at[3])
    pl.semaphore_wait(barrier, 30)

    def rows_of(r):
        return pl.ds(pl.multiple_of(r * 16, 16), 16)

    def send_slices(s):
        for to in peers:
            send(l_panel.at[s, rows_of(to), :], slices[s].at[grp], p1_send.at[s], p1_recv.at[s], leaf, to)
        pltpu.make_async_copy(l_panel.at[s, rows_of(grp), :], slices[s].at[grp], p1_recv.at[s]).start()

    send_slices(0)

    wait(owner, table_sem.at[0])
    wait(structure, table_sem.at[1])
    for s in range(2):
        for j in range(16):
            own_table[s * 16 + j] = owner[structure[s, leaf, j]] >> 2

    def find_k(q, carry):
        for s in range(2):
            k = jnp.int32(0)
            for j in range(16):
                k = jnp.where(own_table[s * 16 + j] == q, j, k)
            k_table[s * 16 + q] = k
        return carry

    lax.fori_loop(0, 16, find_k, 0)
    send_slices(1)

    def find_block(i, carry):
        for s in range(2):
            row, col = jnp.int32(0), jnp.int32(0)
            for j in range(16):
                slot = owner[structure[s, i, j]]
                held_by, pick = slot >> 2, slot & 3
                row = jnp.where(held_by == leaf, pick, row)
                col = jnp.where(held_by == grp, pick, col)
            block_table[s * 16 + i] = row * 4 + col
        return carry

    for s in range(2):
        wait(slices[s], p1_recv.at[s])
        for q in range(16):
            stage[s, q] = slices[s][k_table[s * 16 + q]]
        for to in peers:
            send(stage.at[s, to], panels.at[leaf, s, grp], p2_send.at[s], p2_recv.at[s], leaf, to)
        pltpu.make_async_copy(stage.at[s, grp], panels.at[leaf, s, grp], p2_recv.at[s]).start()

    lax.fori_loop(0, 16, find_block, 0)
    wait(blocks, in_sem)

    def place_of(u):
        pair, turn = div(u + 2, 4), rem(u + 2, 4)
        m = jnp.where(u < 2, 0, jnp.where(u < 14, 2 * pair - 1 + rem(turn, 2), 7))
        s = jnp.where(u < 2, u, jnp.where(u < 14, div(turn, 2), u - 14))
        from_z = rem(z + 8 + jnp.where(rem(m, 2) == 1, -div(m + 1, 2), div(m, 2)), 8)
        return m, s, from_z

    def peer(along, d):
        return rem(y + along * d, 4) * 4 + rem(x + (1 - along) * d, 4)

    def place(along):
        return x * (1 - along) + y * along

    def multiply(u, s, from_leaf, e):
        along = rem(u, 2)
        block = blocks[block_table[s * 16 + from_leaf]]
        panel = panels[from_leaf, s].reshape(256, 256)
        product = jnp.dot(block, panel, preferred_element_type=F32).astype(BF16)
        for q in range(16):
            to = (q % 4) * (1 - along) + (q // 4) * along
            sub = (q // 4) * (1 - along) + (q % 4) * along
            products[u, to, div(sub, 2), e, rem(sub, 2)] = product[q * 16 : q * 16 + 16, :]

    def gather(u, h):
        m, s, from_z = place_of(u)
        held = panels.at[2 * from_z + core, s]
        if h == 0:
            pl.when(m == 0)(lambda: wait(held, p2_recv.at[s]))
        half = held.at[pl.ds(h * 8, 8)]
        pl.when(m > 0)(lambda: wait(half, ring_recv.at[m * 4 + s * 2 + h]))
        up = (m == 0) | ((rem(m, 2) == 1) & (m <= (5 if h == 0 else 3)))
        down = (m == 0) | ((rem(m, 2) == 0) & (m <= (4 if h == 0 else 6)))

        @pl.when(up)
        def _():
            slot = jnp.where(m == 0, 1, m + 2)
            send(half, half, ring_send, ring_recv.at[slot * 4 + s * 2 + h], rem(z + 1, 8) * 2 + core, grp)

        @pl.when(down)
        def _():
            slot = jnp.where(m == 0, 2, jnp.minimum(m + 2, 7))
            send(half, half, ring_send, ring_recv.at[slot * 4 + s * 2 + h], rem(z + 7, 8) * 2 + core, grp)

        send(half, half, sib_send, sib_recv.at[u], 2 * z + 1 - core, grp)

    def multiply_own(u):
        m, s, from_z = place_of(u)
        multiply(u, s, 2 * from_z + core, 0)

    def is_direct(u):
        return (u < EARLY) | (u >= DIRECT)

    def multiply_other(u):
        m, s, from_z = place_of(u)
        from_leaf = 2 * from_z + 1 - core
        wait(panels.at[from_leaf, s], sib_recv.at[u])
        multiply(u, s, from_leaf, 1)
        along = rem(u, 2)
        opposite = rem(place(along) + 2, 4)

        @pl.when(~is_direct(u))
        def _():
            send(products.at[u, opposite, 0], halves.at[u, 0], half_send, half_recv.at[u], leaf, peer(along, 1))
            send(products.at[u, opposite, 1], halves.at[u, 1], half_send, half_recv.at[u], leaf, peer(along, 3))

        @pl.when(is_direct(u))
        def _():
            for d, slot in ((2, 2), (1, 0), (3, 1)):
                to = rem(place(along) + d, 4)
                send(products.at[u, to], sums.at[u, slot], sum_send, sum_recv.at[u], leaf, peer(along, d))

    def add_halves(u):
        along = rem(u, 2)
        after, before = rem(place(along) + 1, 4), rem(place(along) + 3, 4)
        wait(halves.at[u], half_recv.at[u])
        products[u, after, 0] = (products[u, after, 0].astype(F32) + halves[u, 0].astype(F32)).astype(BF16)
        send(products.at[u, after], sums.at[u, 0], sum_send_two, sum_recv.at[u], leaf, peer(along, 1))
        products[u, before, 1] = (products[u, before, 1].astype(F32) + halves[u, 1].astype(F32)).astype(BF16)
        send(products.at[u, before], sums.at[u, 1], sum_send_two, sum_recv.at[u], leaf, peer(along, 3))

    def add_sums(u, received):
        along = rem(u, 2)
        wait(sums.at[u, pl.ds(0, received)], sum_recv.at[u])
        total = products[u, place(along)].astype(F32)
        for slot in range(received):
            total = total + sums[u, slot].astype(F32)
        total = total.astype(BF16)
        for to in range(4):
            for e in range(2):
                parts[u, to, e] = total[to // 2, e, to % 2]
        for d in (2, 1, 3):
            to = rem(place(1 - along) + d, 4)
            send(parts.at[u, to], parts_in.at[u, d - 1], part_send, part_recv.at[u], leaf, peer(1 - along, d))

    def add_parts(u):
        m, s, from_z = place_of(u)
        wait(parts_in.at[u], part_recv.at[u])
        total = parts[u, place(1 - rem(u, 2))].astype(F32)
        for d in range(3):
            total = total + parts_in[u, d].astype(F32)
        finals[u] = (-total).astype(BF16)

        def send_rows(s):
            @pl.when(m == 0)
            def _():
                pltpu.make_async_copy(finals.at[u, 0], rows[s].at[leaf], row_recv.at[s]).start()

            @pl.when(m > 0)
            def _():
                send(finals.at[u, 0], rows[s].at[leaf], row_send, row_recv.at[s], 2 * from_z + core, grp)

            send(finals.at[u, 1], rows[s].at[leaf], row_send, row_recv.at[s], 2 * from_z + 1 - core, grp)

        pl.when(s == 0)(lambda: send_rows(0))
        pl.when(s == 1)(lambda: send_rows(1))

    def step(t, carry):
        both = range(2)

        def halves_stage():
            @pl.when((t >= LAG_HALVES) & (t < 8 + LAG_HALVES))
            def _():
                for i in both:
                    u = 2 * (t - LAG_HALVES) + i
                    pl.when(~is_direct(u))(lambda: add_halves(u))

        def sums_stage():
            @pl.when((t >= LAG_SUMS) & (t < 8 + LAG_SUMS))
            def _():
                for i in both:
                    pair = t - LAG_SUMS
                    pair = jnp.where(pair == 6, 7, jnp.where(pair == 7, 6, pair))
                    u = 2 * pair + i
                    pl.when(~is_direct(u))(lambda: add_sums(u, 2))
                    pl.when(is_direct(u))(lambda: add_sums(u, 3))

        def parts_stage():
            @pl.when(t >= LAG_PARTS)
            def _():
                for i in both:
                    u = 2 * (t - LAG_PARTS) + i
                    u = jnp.where(u == 12, 14, jnp.where((u == 13) | (u == 14), u - 1, u))
                    add_parts(u)

        @pl.when(t < 8)
        def _():
            for i in both:
                for h in both:
                    gather(2 * t + i, h)
            for i in both:
                multiply_own(2 * t + i)
                multiply_other(2 * t + i)

        sums_stage()
        halves_stage()
        parts_stage()

        return carry

    lax.fori_loop(0, 8 + LAG_PARTS, step, 0)

    def send_end(kind, s):
        sem = end_recv.at[kind * (1 + s)]
        for to in peers:
            send(leaving.at[kind, s, to], arriving.at[kind, s, grp], end_send, sem, leaf, to)
        pltpu.make_async_copy(leaving.at[kind, s, grp], arriving.at[kind, s, grp], sem).start()

    def diag_part(s):
        value = lax.dot_general(
            slices[s][...].reshape(256, 256), leaving[0, s].reshape(256, 256), (((0,), (0,)), ((), ())),
            preferred_element_type=F32,
        )
        leaving[1, s] = value.astype(BF16).reshape(16, 16, 256)
        send_end(1, s)

    for s in range(2):
        wait(rows[s], row_recv.at[s])
        for j in range(16):
            leaving[0, s, j] = rows[s][own_table[s * 16 + j]]
        send_end(0, s)
        diag_part(s)

    wait(diag_inverse, table_sem.at[2])
    wait(arriving.at[0], end_recv.at[0])
    pltpu.make_async_copy(arriving.at[0], off_out, table_sem.at[0]).start()
    for s in range(2):
        wait(arriving.at[1, s], end_recv.at[1 + s])
        total = arriving[1, s, 0].astype(F32)
        for g in range(1, 16):
            total = total + arriving[1, s, g].astype(F32)
        diag_out[s] = diag_inverse[s] - total

    pltpu.make_async_copy(arriving.at[0], off_out, table_sem.at[0]).wait()

    for s in range(2):
        wait(slices[s].at[pl.ds(0, 15)], p1_send.at[s])
        wait(stage.at[s, pl.ds(0, 15)], p2_send.at[s])
    wait(leaving.at[:, :, pl.ds(0, 15)], end_send)
    wait(panels.at[pl.ds(0, 7)], ring_send)
    wait(panels.at[pl.ds(0, 8)], sib_send)
    wait(halves.at[pl.ds(0, DIRECT - EARLY)], half_send)
    wait(sums.at[pl.ds(0, DIRECT - EARLY), pl.ds(0, 2)], sum_send_two)
    wait(sums.at[pl.ds(0, 16 - DIRECT + EARLY)], sum_send)
    wait(parts_in, part_send)
    wait(finals.at[pl.ds(0, 15)], row_send)


def finish(off, diag, off_out, diag_out):
    off_out[...] = off[...]
    diag_out[...] = diag[...]


def per_device(kept_inverse, owner_map, structure, l_panel, diag_inverse):
    hbm = pl.BlockSpec(memory_space=pl.ANY)
    vmem = pl.BlockSpec(memory_space=pltpu.VMEM)
    dma = pltpu.SemaphoreType.DMA
    off, diag = pl.pallas_call(
        kernel,
        out_shape=(
            jax.ShapeDtypeStruct((2, 16, 16, 256), BF16),
            jax.ShapeDtypeStruct((2, 16, 256), F32),
        ),
        in_specs=[hbm] * 5,
        out_specs=(hbm, vmem),
        scratch_shapes=[
            pltpu.VMEM((16, 256, 256), BF16),
            pltpu.VMEM((16, 16, 256), BF16),
            pltpu.VMEM((16, 16, 256), BF16),
            pltpu.VMEM((2, 16, 16, 256), BF16),
            pltpu.VMEM((16, 2, 16, 16, 256), BF16),
            pltpu.VMEM((16, 4, 2, 2, 2, 16, 256), BF16),
            pltpu.VMEM((16, 2, 2, 2, 16, 256), BF16),
            pltpu.VMEM((16, 3, 2, 2, 2, 16, 256), BF16),
            pltpu.VMEM((16, 4, 2, 16, 256), BF16),
            pltpu.VMEM((16, 3, 2, 16, 256), BF16),
            pltpu.VMEM((16, 2, 16, 256), BF16),
            pltpu.VMEM((16, 16, 256), BF16),
            pltpu.VMEM((16, 16, 256), BF16),
            pltpu.VMEM((2, 2, 16, 16, 256), BF16),
            pltpu.VMEM((2, 2, 16, 16, 256), BF16),
            pltpu.VMEM((2, 256, 256), BF16),
            pltpu.VMEM((2, 16, 256), F32),
            pltpu.SMEM((64,), jnp.int32),
            pltpu.SMEM((2, 16, 16), jnp.int32),
            pltpu.SMEM((32,), jnp.int32),
            pltpu.SMEM((32,), jnp.int32),
            pltpu.SMEM((32,), jnp.int32),
            dma, dma((4,)), dma((2,)), dma((2,)), dma((2,)), dma((2,)),
            dma, dma((32,)), dma, dma((16,)),
            dma, dma((16,)), dma, dma, dma((16,)), dma, dma((16,)),
            dma, dma((2,)), dma, dma((3,)),
        ],
        compiler_params=pltpu.CompilerParams(
            collective_id=0, has_side_effects=True, vmem_limit_bytes=VMEM_LIMIT
        ),
    )(owner_map, structure, kept_inverse, l_panel, diag_inverse)
    shapes = (jax.ShapeDtypeStruct(off.shape, off.dtype), jax.ShapeDtypeStruct(diag.shape, diag.dtype))
    off, diag = pl.pallas_call(
        finish, out_shape=shapes, in_specs=[vmem, vmem], out_specs=(vmem, vmem)
    )(off, diag)
    return off.reshape(2, 256, 256), diag


def solution(mesh):
    in_specs = (
        P("leaf", "grp"),
        P(),
        P(),
        P(None, ("leaf", "grp"), None),
        P(None, ("leaf", "grp"), None),
    )
    out_specs = (P(None, ("leaf", "grp"), None), P(None, ("leaf", "grp"), None))
    return jax.shard_map(
        per_device, mesh=mesh, in_specs=in_specs, out_specs=out_specs, check_vma=False
    )
```
